256 devices in a mesh: wide: 32 (over y, z), narrow: 8 (over x, core).
Axes of the slice: x: 4, y: 4, z: 8, core: 2. Of those that a mesh axis runs over, the one named last changes fastest.
Arguments:
- density_blocks: float32 [6144, 128, 128], P(('wide', 'narrow')), may hold values from -0.4 to 0.4
- block_groups: int32 [6144, 2], P(('wide', 'narrow')), may hold values from 0 to 63
- block_brick: int32 [6144], P(('wide', 'narrow')), may hold values from 0 to 32767, as said below
- orbital_freq: float32 [3, 8192], replicated, may hold values from 0.1 to 2
- orbital_phase: float32 [3, 8192], replicated, may hold values from -3.140625 to 3.140625
- core_density: float32 [32, 1024, 1024], P('wide', None, 'narrow'), may hold values from 0.2 to 2
Outputs:
- xc_spectrum: float32 [32, 2, 1024, 512], P('wide', None, 'narrow')
The draws below stay inside these ranges and needn't reach their ends.
Inputs may be any that keep to these rules, and one draw needn't show every extreme that they name: `block_brick`: every block stored on the device of narrow index n has its brick within the columns n * 1024 / 8 to (n + 1) * 1024 / 8 - 1 of the grid. The blocks of one device have at most 2 bricks, counted with repeats, in the planes of any one index of wide, and some device has exactly 2.
All inputs are finite; a program needn't handle non-finite values.
Results may differ from the reference program's by a relative error of at most 0.0003.
Values sent between devices are 32-bit elements; how exact they have to be, the bound alone decides.
A program may use at most 64 MiB of HBM per device.

```python
import math
import jax
import jax.numpy as jnp
from jax import lax

NX = 1024
NY = 1024
GRP = 128
BY = 32
BX = 32
NGRP = 64
BLK_DEV = 24
Z_DEV = 1
NORB = 8192
NZ = 32
NBLK = 6144
N_WIDE = 32
N_NARROW = 8


def draw_block_brick(key, part):
    base_key = jax.random.fold_in(key, 11)
    row_keys = jax.random.split(base_key, N_NARROW)
    profile = jnp.array([2 * BLK_DEV, BLK_DEV, BLK_DEV // 2, BLK_DEV // 2], jnp.int32)
    row_loads = jnp.tile(profile, N_WIDE // 4)
    column_bricks = NX // N_NARROW // BX

    def one_row(row_key, row_index):
        keys_four = jax.random.split(row_key, 4)
        home_order = jax.random.permutation(keys_four[0], N_WIDE)
        home_loads = jnp.zeros((N_WIDE,), jnp.int32).at[home_order].set(row_loads)
        bounds = jnp.cumsum(home_loads)
        positions = jnp.arange(N_WIDE * BLK_DEV, dtype=jnp.int32)
        home_index = jnp.searchsorted(bounds, positions, side='right').astype(jnp.int32)
        total = N_WIDE * BLK_DEV
        plane_index = home_index * Z_DEV + jax.random.randint(keys_four[1], (total,), 0, Z_DEV)
        row_block = jax.random.randint(keys_four[2], (total,), 0, NY // BY)
        column_block = row_index * column_bricks + jax.random.randint(keys_four[3], (total,), 0, column_bricks)
        brick_ids = (plane_index * (NY // BY) + row_block) * (NX // BX) + column_block
        return brick_ids.reshape(BLK_DEV, N_WIDE).T
    row_bricks = jax.vmap(one_row)(row_keys, jnp.arange(N_NARROW, dtype=jnp.int32))
    return jnp.transpose(row_bricks, (1, 0, 2)).reshape(-1).astype(jnp.int32)


def set_ends(drawn, own_key, least, largest):
    index_at = [jax.random.randint(jax.random.fold_in(own_key, axis), (), 0, length) for axis, length in enumerate(drawn.shape)]
    main_axis = drawn.shape.index(max(drawn.shape))
    next_to = index_at[:main_axis] + [(index_at[main_axis] + 1) % drawn.shape[main_axis]] + index_at[main_axis + 1:]
    return drawn.at[tuple(index_at)].set(least).at[tuple(next_to)].set(largest)


def level_of(rng, extent, cuts, smallest, top_value):
    factor_of = 1.0
    for axis_at, blocks in cuts:
        heights = jax.random.uniform(jax.random.fold_in(jax.random.fold_in(rng, 6), axis_at), (blocks,), jnp.float32, smallest / len(cuts), top_value / len(cuts))
        factor_of = factor_of * jnp.repeat(jnp.exp(heights), extent[axis_at] // blocks).reshape((-1,) + (1,) * (len(extent) - 1 - axis_at))
    return factor_of


def scatter_about(stream_key, extent, scale, reach, shards=(), kind=jnp.bfloat16):
    factor_of = level_of(stream_key, extent, shards, -0.22, 0.18) if shards else 1.0
    entries = jax.random.normal(stream_key, extent, jnp.float32) * scale * factor_of
    return jnp.minimum(jnp.maximum(entries, -reach), reach).astype(kind)


def setup_inputs(seed: int = 0) -> dict:
    seeds = jax.random.split(jax.random.key(seed), 7)
    density_blocks = scatter_about(seeds[0], (NBLK, GRP, GRP), 0.06, 0.4, ((0, 256),), jnp.float32)
    block_groups = set_ends(jax.random.randint(seeds[1], (NBLK, 2), 0, NGRP), jax.random.fold_in(seeds[1], 1), 0, NGRP - 1).astype(jnp.int32)
    block_brick = draw_block_brick(jax.random.fold_in(seeds[6], 71), 0)
    orbital_freq = jnp.clip(jax.random.uniform(seeds[3], (3, NORB), jnp.float32, 0.1, 2.0), 0.1, 2.0)
    orbital_phase = jnp.clip(jax.random.uniform(seeds[4], (3, NORB), jnp.float32, -3.140625, 3.140625), -3.140625, 3.140625)
    core_density = jnp.clip(jnp.exp(math.log(2.0) - 2.3025851 * jax.random.uniform(seeds[5], (NZ, NY, NX), jnp.float32) ** level_of(seeds[5], (NZ, NY, NX), ((0, 32), (2, 8)), -0.2, 0.2)), 0.2, 2.0)
    return {"density_blocks": density_blocks, "block_groups": block_groups, "block_brick": block_brick, "orbital_freq": orbital_freq, "orbital_phase": orbital_phase, "core_density": core_density}


energy_coef = -0.75 * (3.0 / math.pi) ** (1.0 / 3.0)

def brick_pieces(blocks, group_pairs, brick_ids, orbital_freq, orbital_phase):
    row_bricks = NX // BX
    col_bricks = NY // BY
    column_block = brick_ids % row_bricks
    remainder = brick_ids // row_bricks
    row_block = remainder % col_bricks
    plane_index = remainder // col_bricks
    freq_groups = orbital_freq.reshape(3, -1, GRP)
    shift_groups = orbital_phase.reshape(3, -1, GRP)
    y_cells = (row_block * BY)[:, None] + jnp.arange(BY, dtype=jnp.int32)[None, :]
    x_cells = (column_block * BX)[:, None] + jnp.arange(BX, dtype=jnp.int32)[None, :]

    def orbital_values(group_ids):
        frequency = jnp.take(freq_groups, group_ids, axis=1)
        phase_shift = jnp.take(shift_groups, group_ids, axis=1)
        along_y = jnp.cos(y_cells.astype(jnp.float32)[:, :, None] * frequency[1][:, None, :] + phase_shift[1][:, None, :])
        along_x = jnp.cos(x_cells.astype(jnp.float32)[:, :, None] * frequency[0][:, None, :] + phase_shift[0][:, None, :])
        along_z = jnp.cos(plane_index.astype(jnp.float32)[:, None] * frequency[2] + phase_shift[2])
        orbital_table = along_y[:, :, None, :] * along_x[:, None, :, :] * along_z[:, None, None, :]
        return orbital_table.reshape(group_ids.shape[0], BY * BX, GRP)
    left_values = orbital_values(group_pairs[:, 0])
    right_values = orbital_values(group_pairs[:, 1])
    mixed_rows = jnp.einsum('sci,sij->scj', left_values, blocks, precision=lax.Precision.HIGHEST, preferred_element_type=jnp.float32)
    return lax.optimization_barrier(jnp.sum(mixed_rows * right_values, axis=2))

def reference(density_blocks, block_groups, block_brick, orbital_freq, orbital_phase, core_density):
    step_size = math.gcd(BLK_DEV, 8)
    blocks = density_blocks.reshape(-1, step_size, GRP, GRP)
    group_sets = block_groups.reshape(-1, step_size, 2)
    brick_sets = block_brick.reshape(-1, step_size)

    def one_batch(inputs):
        return brick_pieces(inputs[0], inputs[1], inputs[2], orbital_freq, orbital_phase)
    pieces = lax.map(one_batch, (blocks, group_sets, brick_sets)).reshape(-1, BY * BX)
    brick_total = NZ * (NY // BY) * (NX // BX)
    valence = jnp.zeros((brick_total, BY * BX), jnp.float32).at[block_brick].add(pieces)
    valence = valence.reshape(NZ, NY // BY, NX // BX, BY, BX).transpose(0, 1, 3, 2, 4).reshape(NZ, NY, NX)
    rho_total = core_density + valence
    energy = energy_coef * (rho_total * jnp.cbrt(rho_total) - core_density * jnp.cbrt(core_density))
    half_x = jnp.fft.rfft(energy, axis=2)[:, :, :NX // 2]
    spectrum = jnp.fft.fft(half_x, axis=1) / math.sqrt(NX * NY)
    stacked = jnp.stack([jnp.real(spectrum), jnp.imag(spectrum)], axis=1)
    return stacked.astype(jnp.float32)
```

```python
import functools
import math

import jax
import jax.numpy as jnp
import ml_dtypes
import numpy as np
from jax import lax
from jax.experimental import pallas as pl
from jax.experimental.pallas import tpu as pltpu
from jax.sharding import PartitionSpec as P

NX = 1024
NY = 1024
GRP = 128
BY = 32
BX = 32
MESH = pl.DeviceIdType.MESH

energy_coef = -0.75 * (3.0 / math.pi) ** (1.0 / 3.0)

INV_TURN = 1.0 / (2.0 * math.pi)
PI_HI = 3.140625
PI_LO = math.pi - PI_HI
SINE = (
    2.604579135698264e-06,
    -0.00019808792785020506,
    0.008333047269825162,
    -0.16666657833027024,
    0.9999999956345141,
)


def cosine(angle):
    turns = jnp.round(angle * INV_TURN)
    half = (0.5 * angle - turns * PI_HI) - turns * PI_LO
    square = half * half
    poly = SINE[0]
    for coef in SINE[1:]:
        poly = poly * square + coef
    sine = half * poly
    return 1.0 - 2.0 * (sine * sine)


def split(value):
    high = value.astype(jnp.bfloat16)
    return high, (value - high.astype(jnp.float32)).astype(jnp.bfloat16)


def power43(value):
    return jnp.exp(jnp.log(value) * (4.0 / 3.0))


def split_table(table):
    table = np.asarray(table, np.float32)
    high = table.astype(ml_dtypes.bfloat16)
    low = (table - high.astype(np.float32)).astype(ml_dtypes.bfloat16)
    return np.stack([high, low])


def y_tables(parts):
    rows = NY // parts
    col = np.arange(NY // 2)
    y = (col % 16) * 32 + (col // 16 % 4) * 8 + col // 64
    ky = (
        np.arange(parts)[:, None, None] * rows
        + np.arange(2)[None, :, None]
        + 2 * np.arange(rows // 2)[None, None, :]
    )
    angle = 2.0 * np.pi / NY * (ky[..., None] * y % NY)
    return split_table(
        np.concatenate([np.cos(angle), -np.sin(angle)], 2) / math.sqrt(NY)
    )


def x_tables(chips):
    x = np.arange(NX).reshape(chips, NX // chips)
    kx = np.arange(NX // 2)
    angle = 2.0 * np.pi / NX * (x[..., None] * kx % NX)
    return split_table(
        np.concatenate([np.cos(angle), np.sin(angle)], 1) / math.sqrt(NX)
    )


def one_piece(b, groups_ref, brick_ref, waves_ref, block):
    brick = brick_ref[b]
    x0 = ((brick & 31) * BX).astype(jnp.float32)
    y0 = (((brick >> 5) & 31) * BY).astype(jnp.float32)
    z0 = (brick >> 10).astype(jnp.float32)
    step = lax.broadcasted_iota(jnp.int32, (32, GRP), 0).astype(jnp.float32)
    xs, ys = step + x0, step + y0

    def tables(side):
        wave = waves_ref[groups_ref[b, side]]
        along_x = cosine(xs * wave[0:1] + wave[3:4])
        along_y = cosine(ys * wave[1:2] + wave[4:5])
        along_z = cosine(z0 * wave[2:3] + wave[5:6])
        return along_x * along_z, along_y

    left_x, left_y = tables(0)
    right_x, right_y = tables(1)
    high, low = split(block)
    weights = jnp.concatenate(
        [
            jnp.concatenate([high, low], 1),
            jnp.concatenate([high, jnp.zeros_like(low)], 1),
        ],
        0,
    )
    lane = lax.broadcasted_iota(jnp.int32, (32, 8, 128), 2)
    at_x = lax.broadcasted_iota(jnp.int32, (32, 8, 128), 0)
    total = jnp.zeros((8, 128), jnp.float32)
    for part in range(4):
        rows = slice(part * 8, part * 8 + 8)
        left = (left_x[:, None, :] * left_y[None, rows, :]).reshape(256, GRP)
        right = right_x[:, None, :] * right_y[None, rows, :]
        mixed = jnp.dot(
            jnp.concatenate(split(left), 1), weights, preferred_element_type=jnp.float32
        )
        mixed = (mixed[:, :GRP] + mixed[:, GRP:]).reshape(32, 8, GRP) * right
        sums = jnp.sum(mixed, axis=2, keepdims=True)
        total = total + jnp.sum(
            jnp.where(lane == at_x + part * 32, sums, 0.0), axis=0
        )
    return total


def whole_kernel(
    n_wide,
    n_narrow,
    n_blocks,
    groups_ref,
    brick_ref,
    freq_ref,
    phase_ref,
    blocks_hbm,
    core_hbm,
    ytab_hbm,
    xtab_hbm,
    out_ref,
    blocks_ref,
    core_ref,
    ytab_ref,
    xtab_ref,
    waves_ref,
    brick_col,
    piece_ref,
    place_send,
    place_recv,
    send_ref,
    recv_ref,
    core_pow,
    fold_ref,
    half_send,
    half_recv,
    acc_ref,
    load_sem,
    place_ssem,
    place_rsem,
    piece_ssem,
    piece_rsem,
    half_ssem,
    half_rsem,
):
    wide, narrow = lax.axis_index("wide"), lax.axis_index("narrow")
    loads = [
        pltpu.make_async_copy(src, dst, load_sem.at[i])
        for i, (src, dst) in enumerate(
            (
                (blocks_hbm, blocks_ref),
                (core_hbm, core_ref),
                (ytab_hbm, ytab_ref),
                (xtab_hbm, xtab_ref),
            )
        )
    ]
    for load in loads:
        load.start()

    barrier = pltpu.get_barrier_semaphore()

    def greet_wide(d, carry):
        peer = lax.rem(wide + d, n_wide)
        pl.semaphore_signal(
            barrier, inc=1, device_id=(peer, narrow), device_id_type=MESH
        )
        return carry

    def greet_narrow(d, carry):
        peer = lax.rem(narrow + d, n_narrow)
        pl.semaphore_signal(
            barrier, inc=1, device_id=(wide, peer), device_id_type=MESH
        )
        return carry

    lax.fori_loop(1, n_wide, greet_wide, 0)
    lax.fori_loop(1, n_narrow, greet_narrow, 0)

    brick_col[...] = jnp.zeros_like(brick_col)

    def spread(b, carry):
        brick_col[pl.ds(b, 1), :] = jnp.full((1, 128), brick_ref[b], jnp.int32)
        return carry

    lax.fori_loop(0, n_blocks, spread, 0)
    bricks = brick_col[...]
    row = lax.broadcasted_iota(jnp.int32, (128, 128), 0)
    lane = lax.broadcasted_iota(jnp.int32, (128, 128), 1)
    home = jnp.where(row < n_blocks, bricks // 1024, -1)
    home_t = jnp.transpose(home.astype(jnp.float32)).astype(jnp.int32)
    rank = jnp.sum(
        jnp.where((home == home_t) & (lane < row), 1.0, 0.0), axis=1, keepdims=True
    ).astype(jnp.int32)
    slot = jnp.where(row < n_blocks, 2 * home + rank, -1)
    slot_t = jnp.transpose(slot.astype(jnp.float32)).astype(jnp.int32)
    place = (bricks % 4 * 32 + bricks // 32 % 32 + 1).astype(jnp.bfloat16)
    wide_row = lax.broadcasted_iota(jnp.int32, (n_wide * 8, 128), 0)
    wanted = jnp.where(wide_row % 8 < 2, wide_row // 8 * 2 + wide_row % 8, -2)
    pick8 = jnp.where(
        jnp.broadcast_to(slot_t[0:1], (n_wide * 8, 128)) == wanted, 1.0, 0.0
    ).astype(jnp.bfloat16)
    place_send[...] = (
        jnp.dot(pick8, place, preferred_element_type=jnp.float32) - 1.0
    )
    slot_row = lax.broadcasted_iota(jnp.int32, (2 * n_wide, 128), 0)
    pick = jnp.where(
        jnp.broadcast_to(slot_t[0:1], (2 * n_wide, 128)) == slot_row, 1.0, 0.0
    ).astype(jnp.bfloat16)[:, :32]
    pick = jnp.concatenate([pick, pick], 1)

    pl.semaphore_wait(barrier, n_wide + n_narrow - 2)

    def place_copy(d):
        peer = lax.rem(wide + d, n_wide)
        return pltpu.make_async_remote_copy(
            src_ref=place_send.at[pl.ds(pl.multiple_of(peer * 8, 8), 8)],
            dst_ref=place_recv.at[pl.ds(pl.multiple_of(wide * 8, 8), 8)],
            send_sem=place_ssem.at[d],
            recv_sem=place_rsem.at[d],
            device_id=(peer, narrow),
            device_id_type=MESH,
        )

    def start_place(d, carry):
        place_copy(d).start()
        return carry

    lax.fori_loop(1, n_wide, start_place, 0)
    own8 = pl.ds(pl.multiple_of(wide * 8, 8), 8)
    place_recv[own8] = place_send[own8]

    for g in range(waves_ref.shape[0]):
        at = slice(g * GRP, g * GRP + GRP)
        waves_ref[g, 0:3, :] = freq_ref[:, at]
        waves_ref[g, 3:6, :] = phase_ref[:, at]
        waves_ref[g, 6:8, :] = jnp.zeros((2, GRP), jnp.float32)
    loads[0].wait()
    piece_ref[...] = jnp.zeros_like(piece_ref)

    def work(b, carry):
        piece_ref[pl.ds(pl.multiple_of(b * 8, 8), 8), :] = one_piece(
            b, groups_ref, brick_ref, waves_ref, blocks_ref[b]
        )
        return carry

    lax.fori_loop(0, n_blocks, work, 0)
    for r in range(8):
        high, low = split(piece_ref[pl.ds(r, 32, stride=8), :])
        send_ref[pl.ds(r, 2 * n_wide, stride=8), :] = jnp.dot(
            pick, jnp.concatenate([high, low], 0), preferred_element_type=jnp.float32
        )

    def piece_copy(d):
        peer = lax.rem(wide + d, n_wide)
        return pltpu.make_async_remote_copy(
            src_ref=send_ref.at[pl.ds(pl.multiple_of(peer * 16, 16), 16)],
            dst_ref=recv_ref.at[pl.ds(pl.multiple_of(wide * 16, 16), 16)],
            send_sem=piece_ssem.at[d],
            recv_sem=piece_rsem.at[d],
            device_id=(peer, narrow),
            device_id_type=MESH,
        )

    def start_piece(d, carry):
        piece_copy(d).start()
        return carry

    lax.fori_loop(1, n_wide, start_piece, 0)
    own16 = pl.ds(pl.multiple_of(wide * 16, 16), 16)
    recv_ref[own16] = send_ref[own16]

    loads[1].wait()
    for r in range(8):
        for part in range(4):
            core_pow[pl.ds((r * 4 + part) * 32, 32), :] = power43(
                core_ref[pl.ds(part * 8 + r, 32, stride=32), :]
            )

    def wait_place(d, carry):
        place_copy(d).wait()
        return carry

    lax.fori_loop(1, n_wide, wait_place, 0)
    brick_lane = lax.broadcasted_iota(jnp.int32, (n_wide, 128), 1).astype(jnp.float32)
    spots = [
        jnp.where(place_recv[pl.ds(k, n_wide, stride=8), :] == brick_lane, 1.0, 0.0)
        for k in range(2)
    ]
    gather = jnp.transpose(jnp.concatenate([*spots, *spots], 0)).astype(jnp.bfloat16)

    def wait_piece(d, carry):
        piece_copy(d).wait()
        return carry

    lax.fori_loop(1, n_wide, wait_piece, 0)
    group = lax.broadcasted_iota(jnp.int32, (32, 128), 1) // 32
    for r in range(8):
        got = jnp.concatenate(
            [recv_ref[pl.ds(k * 8 + r, n_wide, stride=16), :] for k in range(2)], 0
        )
        high, low = split(got)
        sums = jnp.dot(
            gather, jnp.concatenate([high, low], 0), preferred_element_type=jnp.float32
        )
        for part in range(4):
            valence = None
            for c in range(4):
                turned = sums[c * 32 : c * 32 + 32]
                if c != part:
                    turned = pltpu.roll(turned, (c - part) % 4 * 32, 1)
                valence = turned if c == 0 else jnp.where(group == c, turned, valence)
            rho = core_ref[pl.ds(part * 8 + r, 32, stride=32), :] + valence
            energy = energy_coef * (
                power43(jnp.abs(rho)) - core_pow[pl.ds((r * 4 + part) * 32, 32), :]
            )
            for parity in range(2):
                fold = (
                    energy[:16] + energy[16:]
                    if parity == 0
                    else energy[:16] - energy[16:]
                )
                fold_ref[parity, pl.ds((r * 4 + part) * 16, 16), :] = jnp.concatenate(
                    split(fold), 1
                )

    loads[2].wait()
    chips = n_narrow // 2

    def half_copy(i, peer):
        return pltpu.make_async_remote_copy(
            src_ref=half_send.at[peer],
            dst_ref=half_recv.at[narrow],
            send_sem=half_ssem.at[i],
            recv_sem=half_rsem.at[i],
            device_id=(wide, peer),
            device_id_type=MESH,
        )

    hops = [(2, 0), (2, 1), (1, 0), (3, 0), (1, 1), (3, 1), (0, 1), (0, 0)]

    def peer_at(hop):
        chip = lax.rem(narrow // 2 + hop[0], chips)
        return chip * 2 + lax.rem(narrow + hop[1], 2)

    for i, hop in enumerate(hops):
        peer = peer_at(hop)
        target = half_send.at[peer] if hop != (0, 0) else half_recv.at[narrow]
        for parity in range(2):
            spread_y = jnp.dot(
                ytab_ref[0, peer, parity],
                fold_ref[parity],
                preferred_element_type=jnp.float32,
            )
            half = (
                spread_y[:, :128]
                + spread_y[:, 128:]
                + jnp.dot(
                    ytab_ref[1, peer, parity],
                    fold_ref[parity, :, 0:128],
                    preferred_element_type=jnp.float32,
                )
            )
            target[pl.ds(parity, 64, stride=2), :] = half[:64]
            target[pl.ds(128 + parity, 64, stride=2), :] = half[64:]
        if hop != (0, 0):
            half_copy(i, peer).start()

    loads[3].wait()
    waits = {0: (6,), 1: (3, 5), 3: (2, 4), 2: (0, 1)}
    for n, (on, copies) in enumerate(waits.items()):
        for i in copies:
            half_copy(i, peer_at(hops[i])).wait_recv()
        chip = lax.rem(narrow // 2 + on, chips)
        columns = jnp.concatenate([half_recv[2 * chip], half_recv[2 * chip + 1]], 1)
        real, imag = columns[:128], columns[128:]
        high, low = split(
            jnp.concatenate(
                [
                    jnp.concatenate([real, imag], 1),
                    jnp.concatenate([imag, -real], 1),
                ],
                0,
            )
        )
        part = (
            jnp.dot(high, xtab_ref[0, chip], preferred_element_type=jnp.float32)
            + jnp.dot(low, xtab_ref[0, chip], preferred_element_type=jnp.float32)
            + jnp.dot(high, xtab_ref[1, chip], preferred_element_type=jnp.float32)
        )
        if n == 0:
            acc_ref[...] = part
        elif n < 3:
            acc_ref[...] += part
        else:
            total = acc_ref[...] + part
            for c in range(2):
                out_ref[0, c] = total[c * 128 : c * 128 + 128]

    for i in range(len(hops) - 1):
        half_copy(i, peer_at(hops[i])).wait_send()


def local(density_blocks, block_groups, block_brick, orbital_freq, orbital_phase, core_density):
    n_wide, n_narrow = lax.axis_size("wide"), lax.axis_size("narrow")
    n_blocks = density_blocks.shape[0]
    ytab, xtab = y_tables(n_narrow), x_tables(n_narrow // 2)
    vmem = pl.BlockSpec(memory_space=pltpu.VMEM)
    smem = pl.BlockSpec(memory_space=pltpu.SMEM)
    hbm = pl.BlockSpec(memory_space=pl.ANY)
    f32, bf16 = jnp.float32, jnp.bfloat16
    rows = NY // n_narrow
    return pl.pallas_call(
        functools.partial(whole_kernel, n_wide, n_narrow, n_blocks),
        out_shape=jax.ShapeDtypeStruct((1, 2, rows, NX // 2), f32),
        in_specs=[smem, smem, vmem, vmem, hbm, hbm, hbm, hbm],
        out_specs=vmem,
        scratch_shapes=[
            pltpu.VMEM(density_blocks.shape, f32),
            pltpu.VMEM(core_density.shape[1:], f32),
            pltpu.VMEM(ytab.shape, bf16),
            pltpu.VMEM(xtab.shape, bf16),
            pltpu.VMEM((orbital_freq.shape[1] // GRP, 8, GRP), f32),
            pltpu.VMEM((128, 128), jnp.int32),
            pltpu.VMEM((32 * 8, 128), f32),
            pltpu.VMEM((n_wide * 8, 128), f32),
            pltpu.VMEM((n_wide * 8, 128), f32),
            pltpu.VMEM((n_wide * 16, 128), f32),
            pltpu.VMEM((n_wide * 16, 128), f32),
            pltpu.VMEM((NY, 128), f32),
            pltpu.VMEM((2, NY // 2, 256), bf16),
            pltpu.VMEM((n_narrow, 256, 128), f32),
            pltpu.VMEM((n_narrow, 256, 128), f32),
            pltpu.VMEM((256, NX // 2), f32),
            pltpu.SemaphoreType.DMA((4,)),
            pltpu.SemaphoreType.DMA((n_wide,)),
            pltpu.SemaphoreType.DMA((n_wide,)),
            pltpu.SemaphoreType.DMA((n_wide,)),
            pltpu.SemaphoreType.DMA((n_wide,)),
            pltpu.SemaphoreType.DMA((n_narrow,)),
            pltpu.SemaphoreType.DMA((n_narrow,)),
        ],
        compiler_params=pltpu.CompilerParams(
            collective_id=0, has_side_effects=True, vmem_limit_bytes=48 * 2**20
        ),
    )(
        block_groups,
        block_brick,
        orbital_freq,
        orbital_phase,
        density_blocks,
        core_density.reshape(core_density.shape[1:]),
        jnp.asarray(ytab),
        jnp.asarray(xtab),
    )


def solution(mesh):
    return jax.shard_map(
        local,
        mesh=mesh,
        in_specs=(
            P(("wide", "narrow"), None, None),
            P(("wide", "narrow"), None),
            P(("wide", "narrow")),
            P(),
            P(),
            P("wide", None, "narrow"),
        ),
        out_specs=P("wide", None, "narrow", None),
        check_vma=False,
    )
```

```python
import functools
import math

import jax
import jax.numpy as jnp
import ml_dtypes
import numpy as np
from jax import lax
from jax.experimental import pallas as pl
from jax.experimental.pallas import tpu as pltpu
from jax.sharding import PartitionSpec as P

NX = 1024
NY = 1024
GRP = 128
BY = 32
BX = 32
MESH = pl.DeviceIdType.MESH

energy_coef = -0.75 * (3.0 / math.pi) ** (1.0 / 3.0)

INV_TURN = 1.0 / (2.0 * math.pi)
PI_HI = 3.140625
PI_LO = math.pi - PI_HI
SINE = (
    2.604579135698264e-06,
    -0.00019808792785020506,
    0.008333047269825162,
    -0.16666657833027024,
    0.9999999956345141,
)


def cosine(angle):
    turns = jnp.round(angle * INV_TURN)
    half = (0.5 * angle - turns * PI_HI) - turns * PI_LO
    square = half * half
    poly = SINE[0]
    for coef in SINE[1:]:
        poly = poly * square + coef
    sine = half * poly
    return 1.0 - 2.0 * (sine * sine)


def split(value):
    high = value.astype(jnp.bfloat16)
    return high, (value - high.astype(jnp.float32)).astype(jnp.bfloat16)


def power43(value):
    return jnp.exp(jnp.log(value) * (4.0 / 3.0))


def split_table(table):
    table = np.asarray(table, np.float32)
    high = table.astype(ml_dtypes.bfloat16)
    low = (table - high.astype(np.float32)).astype(ml_dtypes.bfloat16)
    return np.stack([high, low])


def y_tables(parts):
    rows = NY // parts
    col = np.arange(NY // 2)
    r, g = col // 128, col // 16 % 8
    y = col % 16 * 32 + g % 4 * 8 + 2 * r + g // 4
    ky = (
        np.arange(parts)[:, None, None] * rows
        + np.arange(2)[None, :, None]
        + 2 * np.arange(rows // 2)[None, None, :]
    )
    angle = 2.0 * np.pi / NY * (ky[..., None] * y % NY)
    return split_table(
        np.concatenate([np.cos(angle), -np.sin(angle)], 2) / math.sqrt(NY)
    )


def x_tables(chips):
    h, chip, core, xb, xi = np.ix_(*map(np.arange, (2, chips, 2, 4, 16)))
    x = (chip * 2 + core) * 128 + xb * 32 + h * 16 + xi
    x = x.reshape(2, chips, 2, 64, 1)
    angle = 2.0 * np.pi / NX * (x * np.arange(NX // 2) % NX)
    both = np.stack([np.cos(angle), np.sin(angle)], 3) / math.sqrt(NX)
    return split_table(both.reshape(2, chips, 256, NX // 2))


def block_tables(b, groups_ref, brick_ref, waves_ref, blocks_ref, factor_ref, weight_ref):
    brick = brick_ref[b]
    x0 = ((brick & 31) * BX).astype(jnp.float32)
    y0 = (((brick >> 5) & 31) * BY).astype(jnp.float32)
    z0 = (brick >> 10).astype(jnp.float32)
    step = lax.broadcasted_iota(jnp.int32, (32, GRP), 0).astype(jnp.float32)
    xs, ys = step + x0, step + y0
    for side in range(2):
        wave = waves_ref[groups_ref[side, b]]
        along_z = cosine(z0 * wave[2:3] + wave[5:6])
        factor_ref[b, 2 * side] = cosine(xs * wave[0:1] + wave[3:4]) * along_z
        factor_ref[b, 2 * side + 1] = cosine(ys * wave[1:2] + wave[4:5])
    high, low = split(blocks_ref[b])
    weight_ref[b] = jnp.concatenate(
        [
            jnp.concatenate([high, low], 1),
            jnp.concatenate([high, jnp.zeros_like(low)], 1),
        ],
        0,
    )


def half_piece(b, h, factor_ref, weight_ref):
    cols = slice(h * 16, h * 16 + 16)
    left_x, right_x = factor_ref[b, 0, cols], factor_ref[b, 2, cols]
    weights = weight_ref[b]
    shape = (2, 16, 8, GRP)
    lane = lax.broadcasted_iota(jnp.int32, shape, 3) & 63
    spot = lax.broadcasted_iota(jnp.int32, shape, 1) + 16 * lax.broadcasted_iota(
        jnp.int32, shape, 0
    )
    total = jnp.zeros((8, 128), jnp.float32)
    for part in range(2):
        rows = slice(part * 16, part * 16 + 16)
        left_y = factor_ref[b, 1, rows].reshape(2, 1, 8, GRP)
        right_y = factor_ref[b, 3, rows].reshape(2, 1, 8, GRP)
        left = (left_x[None, :, None, :] * left_y).reshape(256, GRP)
        right = right_x[None, :, None, :] * right_y
        mixed = jnp.dot(
            jnp.concatenate(split(left), 1), weights, preferred_element_type=jnp.float32
        )
        mixed = (mixed[:, :GRP] + mixed[:, GRP:]).reshape(shape) * right
        sums = jnp.sum(mixed, axis=3, keepdims=True)
        total = total + jnp.sum(
            jnp.where(lane == spot + part * 32, sums, 0.0), axis=(0, 1)
        )
    return total


def whole_kernel(
    n_wide,
    n_narrow,
    n_blocks,
    groups_ref,
    brick_ref,
    freq_hbm,
    phase_hbm,
    blocks_hbm,
    core_hbm,
    ytab_hbm,
    xtab_hbm,
    out_ref,
    freq_ref,
    phase_ref,
    blocks_ref,
    core_ref,
    ytab_ref,
    xtab_ref,
    waves_ref,
    factor_ref,
    weight_ref,
    brick_col,
    piece_ref,
    place_send,
    place_recv,
    send_ref,
    recv_ref,
    core_part,
    core_pow,
    fold_ref,
    half_send,
    half_recv,
    acc_ref,
    load_sem,
    place_ssem,
    place_rsem,
    piece_ssem,
    piece_rsem,
    half_ssem,
    half_rsem,
):
    wide, narrow = lax.axis_index("wide"), lax.axis_index("narrow")
    loads = [
        pltpu.make_async_copy(src, dst, load_sem.at[i])
        for i, (src, dst) in enumerate(
            (
                (freq_hbm, freq_ref),
                (phase_hbm, phase_ref),
                (blocks_hbm, blocks_ref),
                (core_hbm, core_ref),
                (ytab_hbm, ytab_ref),
                (xtab_hbm, xtab_ref),
            )
        )
    ]
    for load in loads:
        load.start()

    barrier = pltpu.get_barrier_semaphore()

    def greet_wide(d, carry):
        peer = lax.rem(wide + d, n_wide)
        pl.semaphore_signal(
            barrier, inc=1, device_id=(peer, narrow), device_id_type=MESH
        )
        return carry

    def greet_narrow(d, carry):
        peer = lax.rem(narrow + d, n_narrow)
        pl.semaphore_signal(
            barrier, inc=1, device_id=(wide, peer), device_id_type=MESH
        )
        return carry

    lax.fori_loop(1, n_wide, greet_wide, 0)
    lax.fori_loop(1, n_narrow, greet_narrow, 0)

    brick_col[...] = jnp.zeros_like(brick_col)

    def spread(b, carry):
        brick_col[pl.ds(b, 1), :] = jnp.full((1, 128), brick_ref[b], jnp.int32)
        return carry

    lax.fori_loop(0, n_blocks, spread, 0)
    bricks = brick_col[...]
    row = lax.broadcasted_iota(jnp.int32, (128, 128), 0)
    lane = lax.broadcasted_iota(jnp.int32, (128, 128), 1)
    home = jnp.where(row < n_blocks, bricks >> 10, -1)
    home_t = jnp.transpose(home.astype(jnp.float32)).astype(jnp.int32)
    rank = jnp.sum(
        jnp.where((home == home_t) & (lane < row), 1.0, 0.0), axis=1, keepdims=True
    ).astype(jnp.int32)
    slot = jnp.where(row < n_blocks, 2 * home + rank, -1)
    slot_t = jnp.transpose(slot.astype(jnp.float32)).astype(jnp.int32)
    by = (bricks >> 5) & 31
    place = ((by >> 4) * 64 + (bricks & 3) * 16 + (by & 15) + 1).astype(jnp.bfloat16)
    wide_row = lax.broadcasted_iota(jnp.int32, (n_wide * 8, 128), 0)
    wanted = jnp.where((wide_row & 7) < 2, (wide_row >> 3) * 2 + (wide_row & 7), -2)
    pick8 = jnp.where(
        jnp.broadcast_to(slot_t[0:1], (n_wide * 8, 128)) == wanted, 1.0, 0.0
    ).astype(jnp.bfloat16)
    place_send[...] = (
        jnp.dot(pick8, place, preferred_element_type=jnp.float32) - 1.0
    )
    slot_row = lax.broadcasted_iota(jnp.int32, (2 * n_wide, 128), 0)
    slot_row = jnp.where(slot_row < n_wide, 2 * slot_row, 2 * (slot_row - n_wide) + 1)
    pick = jnp.where(
        jnp.broadcast_to(slot_t[0:1], (2 * n_wide, 128)) == slot_row, 1.0, 0.0
    ).astype(jnp.bfloat16)[:, :32]
    pick = jnp.concatenate([pick, pick], 1)

    loads[0].wait()
    loads[1].wait()
    for g in range(waves_ref.shape[0]):
        at = slice(g * GRP, g * GRP + GRP)
        waves_ref[g, 0:3, :] = freq_ref[:, at]
        waves_ref[g, 3:6, :] = phase_ref[:, at]
        waves_ref[g, 6:8, :] = jnp.zeros((2, GRP), jnp.float32)
    loads[2].wait()
    piece_ref[...] = jnp.zeros_like(piece_ref)

    def prepare(b, carry):
        block_tables(
            b, groups_ref, brick_ref, waves_ref, blocks_ref, factor_ref, weight_ref
        )
        return carry

    lax.fori_loop(0, n_blocks, prepare, 0, unroll=4)

    first = lax.broadcasted_iota(jnp.int32, (32, 128), 1) < 64

    def place_copy(d):
        peer = lax.rem(wide + d, n_wide)
        return pltpu.make_async_remote_copy(
            src_ref=place_send.at[pl.ds(pl.multiple_of(peer * 8, 8), 8)],
            dst_ref=place_recv.at[pl.ds(pl.multiple_of(wide * 8, 8), 8)],
            send_sem=place_ssem.at[d],
            recv_sem=place_rsem.at[d],
            device_id=(peer, narrow),
            device_id_type=MESH,
        )

    def piece_copy(h, d):
        peer = lax.rem(wide + d, n_wide)
        return pltpu.make_async_remote_copy(
            src_ref=send_ref.at[h, pl.ds(pl.multiple_of(peer * 8, 8), 8)],
            dst_ref=recv_ref.at[h, pl.ds(pl.multiple_of(wide * 8, 8), 8)],
            send_sem=piece_ssem.at[h, d],
            recv_sem=piece_rsem.at[h, d],
            device_id=(peer, narrow),
            device_id_type=MESH,
        )

    own8 = pl.ds(pl.multiple_of(wide * 8, 8), 8)
    for h in range(2):

        def work(b, carry, h=h):
            piece_ref[h, pl.ds(pl.multiple_of(b * 8, 8), 8), :] = half_piece(
                b, h, factor_ref, weight_ref
            )
            return carry

        lax.fori_loop(0, n_blocks, work, 0, unroll=8)
        for r in range(8):
            both = jnp.concatenate(split(piece_ref[h, pl.ds(r, 32, stride=8), :]), 0)
            slots = jnp.dot(pick, both, preferred_element_type=jnp.float32)
            send_ref[h, pl.ds(r, n_wide, stride=8), :] = jnp.where(
                first, slots[:n_wide], slots[n_wide:]
            )
        if h == 0:
            pl.semaphore_wait(barrier, n_wide + n_narrow - 2)

        def start_piece(d, carry, h=h):
            piece_copy(h, d).start()
            return carry

        lax.fori_loop(1, n_wide, start_piece, 0)
        recv_ref[h, own8] = send_ref[h, own8]
        if h == 0:

            def start_place(d, carry):
                place_copy(d).start()
                return carry

            lax.fori_loop(1, n_wide, start_place, 0)
            place_recv[own8] = place_send[own8]

    loads[3].wait()
    at = lax.broadcasted_iota(jnp.int32, (256, 256), 0)
    to = (
        ((at >> 4) & 1) * 128 + (at >> 7) * 64 + ((at >> 5) & 3) * 16 + (at & 15)
    )
    order = jnp.where(
        to == lax.broadcasted_iota(jnp.int32, (256, 256), 1), 1.0, 0.0
    ).astype(jnp.bfloat16)
    for r in range(4):
        rows = []
        for g in range(8):
            y = g % 4 * 8 + 2 * r + g // 4
            rows.append(
                jnp.concatenate(
                    [core_ref[pl.ds(y + t * 512, 16, stride=32), :] for t in range(2)],
                    1,
                )
            )
        value = jnp.concatenate(rows, 0)
        high, rest = value.astype(jnp.bfloat16), value
        rest = rest - high.astype(jnp.float32)
        moved = (
            jnp.dot(high, order, preferred_element_type=jnp.float32)
            + sum(
                jnp.dot(part, order, preferred_element_type=jnp.float32)
                for part in split(rest)
            )
        )
        for h in range(2):
            own = moved[:, h * 128 : h * 128 + 128]
            core_part[h, r * 128 : r * 128 + 128, :] = own
            core_pow[h, r * 128 : r * 128 + 128, :] = power43(own)

    def wait_place(d, carry):
        place_copy(d).wait()
        return carry

    lax.fori_loop(1, n_wide, wait_place, 0)
    brick_lane = lax.broadcasted_iota(jnp.int32, (n_wide, 128), 1).astype(jnp.float32)
    spots = [
        jnp.where(place_recv[pl.ds(k, n_wide, stride=8), :] == brick_lane, 1.0, 0.0)
        for k in range(2)
    ]
    gather = jnp.transpose(jnp.concatenate([*spots, *spots], 0)).astype(jnp.bfloat16)

    chips = n_narrow // 2
    hops = [(2, 0), (2, 1), (1, 0), (3, 0), (1, 1), (3, 1), (0, 1), (0, 0)]

    def peer_at(hop):
        chip = lax.rem(narrow // 2 + hop[0], chips)
        return chip * 2 + lax.rem(narrow + hop[1], 2)

    def half_copy(h, i):
        peer = peer_at(hops[i])
        return pltpu.make_async_remote_copy(
            src_ref=half_send.at[h, peer],
            dst_ref=half_recv.at[h, narrow],
            send_sem=half_ssem.at[h, i],
            recv_sem=half_rsem.at[h, i],
            device_id=(wide, peer),
            device_id_type=MESH,
        )

    group = lax.broadcasted_iota(jnp.int32, (16, 128), 1) >> 4
    low16 = group < 4
    low64 = lax.broadcasted_iota(jnp.int32, (64, 128), 1) < 64
    for h in range(2):

        def wait_piece(d, carry, h=h):
            piece_copy(h, d).wait()
            return carry

        lax.fori_loop(1, n_wide, wait_piece, 0)
        for r in range(4):
            even = recv_ref[h, pl.ds(2 * r, n_wide, stride=8), :]
            odd = recv_ref[h, pl.ds(2 * r + 1, n_wide, stride=8), :]
            got = jnp.concatenate(
                [
                    jnp.where(first, even, pltpu.roll(odd, 64, 1)),
                    jnp.where(first, pltpu.roll(even, 64, 1), odd),
                ],
                0,
            )
            sums = jnp.dot(
                gather,
                jnp.concatenate(split(got), 0),
                preferred_element_type=jnp.float32,
            )
            tiles = [sums[j * 16 : j * 16 + 16] for j in range(8)]
            for bit in (1, 2, 4):
                for j in range(8):
                    if not j & bit:
                        a, b = tiles[j], tiles[j | bit]
                        keep = (group & bit) == 0
                        tiles[j] = jnp.where(keep, a, pltpu.roll(b, 16 * bit, 1))
                        tiles[j | bit] = jnp.where(
                            keep, pltpu.roll(a, 128 - 16 * bit, 1), b
                        )
            for g in range(8):
                at = slice((r * 8 + g) * 16, (r * 8 + g) * 16 + 16)
                rho = core_part[h, at, :] + tiles[g]
                energy = energy_coef * (power43(jnp.abs(rho)) - core_pow[h, at, :])
                other = pltpu.roll(energy, 64, 1)
                fold = jnp.where(low16, energy + other, other - energy)
                high = fold.astype(jnp.bfloat16).astype(jnp.float32)
                rest = fold - high
                fold_ref[h, 0, at, :] = jnp.where(
                    low16, high, pltpu.roll(rest, 64, 1)
                ).astype(jnp.bfloat16)
                fold_ref[h, 1, at, :] = jnp.where(
                    low16, pltpu.roll(high, 64, 1), rest
                ).astype(jnp.bfloat16)
        if h == 0:
            loads[4].wait()
        for i, hop in enumerate(hops):
            peer = peer_at(hop)
            target = half_recv.at[h, narrow] if hop == (0, 0) else half_send.at[h, peer]
            for parity in range(2):
                half = jnp.dot(
                    ytab_ref[0, peer, parity],
                    fold_ref[h, parity],
                    preferred_element_type=jnp.float32,
                ) + jnp.dot(
                    ytab_ref[1, peer, parity],
                    fold_ref[h, parity],
                    preferred_element_type=jnp.float32,
                )
                half = half + pltpu.roll(half, 64, 1)
                target[pl.ds(parity, 64, stride=2), :] = jnp.where(
                    low64, half[:64], half[64:]
                )
            if hop != (0, 0):
                half_copy(h, i).start()

    loads[5].wait()
    low256 = (lax.broadcasted_iota(jnp.int32, (128, 256), 1) & 127) < 64
    waits = {0: (6,), 1: (3, 5), 3: (2, 4), 2: (0, 1)}
    for h in range(2):
        for on, copies in waits.items():
            for i in copies:
                half_copy(h, i).wait_recv()
            chip = lax.rem(narrow // 2 + on, chips)
            ours = [half_recv[h, 2 * chip + core] for core in range(2)]
            turned = [pltpu.roll(own, 64, 1) for own in ours]
            real, imag = jnp.concatenate(ours, 1), jnp.concatenate(turned, 1)
            high, low = split(
                jnp.concatenate([real, jnp.where(low256, imag, -imag)], 0)
            )
            part = (
                jnp.dot(high, xtab_ref[0, h, chip], preferred_element_type=jnp.float32)
                + jnp.dot(low, xtab_ref[0, h, chip], preferred_element_type=jnp.float32)
                + jnp.dot(high, xtab_ref[1, h, chip], preferred_element_type=jnp.float32)
            )
            if (h, on) == (0, 0):
                acc_ref[...] = part
            elif (h, on) != (1, 2):
                acc_ref[...] += part
            else:
                total = acc_ref[...] + part
                for c in range(2):
                    out_ref[0, c] = total[c * 128 : c * 128 + 128]

    for h in range(2):
        for i in range(len(hops) - 1):
            half_copy(h, i).wait_send()


def local(density_blocks, block_groups, block_brick, orbital_freq, orbital_phase, core_density):
    n_wide, n_narrow = lax.axis_size("wide"), lax.axis_size("narrow")
    n_blocks = density_blocks.shape[0]
    ytab, xtab = y_tables(n_narrow), x_tables(n_narrow // 2)
    vmem = pl.BlockSpec(memory_space=pltpu.VMEM)
    smem = pl.BlockSpec(memory_space=pltpu.SMEM)
    hbm = pl.BlockSpec(memory_space=pl.ANY)
    f32, bf16 = jnp.float32, jnp.bfloat16
    rows = NY // n_narrow
    return pl.pallas_call(
        functools.partial(whole_kernel, n_wide, n_narrow, n_blocks),
        out_shape=jax.ShapeDtypeStruct((1, 2, rows, NX // 2), f32),
        in_specs=[smem, smem, hbm, hbm, hbm, hbm, hbm, hbm],
        out_specs=vmem,
        scratch_shapes=[
            pltpu.VMEM(orbital_freq.shape, f32),
            pltpu.VMEM(orbital_phase.shape, f32),
            pltpu.VMEM(density_blocks.shape, f32),
            pltpu.VMEM(core_density.shape[1:], f32),
            pltpu.VMEM(ytab.shape, bf16),
            pltpu.VMEM(xtab.shape, bf16),
            pltpu.VMEM((orbital_freq.shape[1] // GRP, 8, GRP), f32),
            pltpu.VMEM((n_blocks, 4, 32, GRP), f32),
            pltpu.VMEM((n_blocks, 2 * GRP, 2 * GRP), bf16),
            pltpu.VMEM((128, 128), jnp.int32),
            pltpu.VMEM((2, 32 * 8, 128), f32),
            pltpu.VMEM((n_wide * 8, 128), f32),
            pltpu.VMEM((n_wide * 8, 128), f32),
            pltpu.VMEM((2, n_wide * 8, 128), f32),
            pltpu.VMEM((2, n_wide * 8, 128), f32),
            pltpu.VMEM((2, NY // 2, 128), f32),
            pltpu.VMEM((2, NY // 2, 128), f32),
            pltpu.VMEM((2, 2, NY // 2, 128), bf16),
            pltpu.VMEM((2, n_narrow, 128, 128), f32),
            pltpu.VMEM((2, n_narrow, 128, 128), f32),
            pltpu.VMEM((256, NX // 2), f32),
            pltpu.SemaphoreType.DMA((6,)),
            pltpu.SemaphoreType.DMA((n_wide,)),
            pltpu.SemaphoreType.DMA((n_wide,)),
            pltpu.SemaphoreType.DMA((2, n_wide)),
            pltpu.SemaphoreType.DMA((2, n_wide)),
            pltpu.SemaphoreType.DMA((2, n_narrow)),
            pltpu.SemaphoreType.DMA((2, n_narrow)),
        ],
        compiler_params=pltpu.CompilerParams(
            collective_id=0, has_side_effects=True, vmem_limit_bytes=62 * 2**20
        ),
    )(
        block_groups.T,
        block_brick,
        orbital_freq,
        orbital_phase,
        density_blocks,
        core_density.reshape(core_density.shape[1:]),
        jnp.asarray(ytab),
        jnp.asarray(xtab),
    )


def solution(mesh):
    return jax.shard_map(
        local,
        mesh=mesh,
        in_specs=(
            P(("wide", "narrow"), None, None),
            P(("wide", "narrow"), None),
            P(("wide", "narrow")),
            P(),
            P(),
            P("wide", None, "narrow"),
        ),
        out_specs=P("wide", None, "narrow", None),
        check_vma=False,
    )
```

```python
import functools
import math

import jax
import jax.numpy as jnp
import ml_dtypes
import numpy as np
from jax import lax
from jax.experimental import pallas as pl
from jax.experimental.pallas import tpu as pltpu
from jax.sharding import PartitionSpec as P

NX = 1024
NY = 1024
GRP = 128
BY = 32
BX = 32
MESH = pl.DeviceIdType.MESH

energy_coef = -0.75 * (3.0 / math.pi) ** (1.0 / 3.0)

INV_TURN = 1.0 / (2.0 * math.pi)
PI_HI = 3.140625
PI_LO = math.pi - PI_HI
SINE = (
    2.604579135698264e-06,
    -0.00019808792785020506,
    0.008333047269825162,
    -0.16666657833027024,
    0.9999999956345141,
)


def cosine(angle):
    turns = jnp.round(angle * INV_TURN)
    half = (0.5 * angle - turns * PI_HI) - turns * PI_LO
    square = half * half
    poly = SINE[0]
    for coef in SINE[1:]:
        poly = poly * square + coef
    sine = half * poly
    return 1.0 - 2.0 * (sine * sine)


def split(value):
    high = value.astype(jnp.bfloat16)
    return high, (value - high.astype(jnp.float32)).astype(jnp.bfloat16)


def power43(value):
    return jnp.exp(jnp.log(value) * (4.0 / 3.0))


def split_table(table):
    table = np.asarray(table, np.float32)
    high = table.astype(ml_dtypes.bfloat16)
    low = (table - high.astype(np.float32)).astype(ml_dtypes.bfloat16)
    return np.stack([high, low])


def y_tables(parts):
    rows = NY // parts
    col = np.arange(NY // 2)
    r, g = col // 128, col // 16 % 8
    y = col % 16 * 32 + g % 4 * 8 + 2 * r + g // 4
    ky = (
        np.arange(parts)[:, None, None] * rows
        + np.arange(2)[None, :, None]
        + 2 * np.arange(rows // 2)[None, None, :]
    )
    angle = 2.0 * np.pi / NY * (ky[..., None] * y % NY)
    return split_table(
        np.concatenate([np.cos(angle), -np.sin(angle)], 2) / math.sqrt(NY)
    )


def x_tables(chips):
    h, chip, core, xb, xi = np.ix_(*map(np.arange, (2, chips, 2, 4, 16)))
    x = (chip * 2 + core) * 128 + xb * 32 + h * 16 + xi
    x = x.reshape(2, chips, 2, 64, 1)
    angle = 2.0 * np.pi / NX * (x * np.arange(NX // 2) % NX)
    both = np.stack([np.cos(angle), np.sin(angle)], 3) / math.sqrt(NX)
    return split_table(both.reshape(2, chips, 256, NX // 2))


def wait_all(ref, sem):
    pltpu.make_async_copy(ref, ref, sem).wait()


def block_tables(b, groups_ref, brick_ref, waves_ref, blocks_ref, factor_ref, weight_ref):
    brick = brick_ref[b]
    x0 = ((brick & 31) * BX).astype(jnp.float32)
    y0 = (((brick >> 5) & 31) * BY).astype(jnp.float32)
    z0 = (brick >> 10).astype(jnp.float32)
    step = lax.broadcasted_iota(jnp.int32, (32, GRP), 0).astype(jnp.float32)
    xs, ys = step + x0, step + y0
    for side in range(2):
        wave = waves_ref[groups_ref[side, b]]
        along_z = cosine(z0 * wave[2:3] + wave[5:6])
        factor_ref[b, 2 * side] = cosine(xs * wave[0:1] + wave[3:4]) * along_z
        factor_ref[b, 2 * side + 1] = cosine(ys * wave[1:2] + wave[4:5])
    high, low = split(blocks_ref[b])
    weight_ref[b] = jnp.concatenate(
        [
            jnp.concatenate([high, low], 1),
            jnp.concatenate([high, jnp.zeros_like(low)], 1),
        ],
        0,
    )


def half_piece(b, h, factor_ref, weight_ref):
    cols = slice(h * 16, h * 16 + 16)
    left_x, right_x = factor_ref[b, 0, cols], factor_ref[b, 2, cols]
    weights = weight_ref[b]
    shape = (2, 16, 8, GRP)
    lane = lax.broadcasted_iota(jnp.int32, shape, 3) & 63
    spot = lax.broadcasted_iota(jnp.int32, shape, 1) + 16 * lax.broadcasted_iota(
        jnp.int32, shape, 0
    )
    total = jnp.zeros((8, 128), jnp.float32)
    for part in range(2):
        rows = slice(part * 16, part * 16 + 16)
        left_y = factor_ref[b, 1, rows].reshape(2, 1, 8, GRP)
        right_y = factor_ref[b, 3, rows].reshape(2, 1, 8, GRP)
        left = (left_x[None, :, None, :] * left_y).reshape(256, GRP)
        right = right_x[None, :, None, :] * right_y
        mixed = jnp.dot(
            jnp.concatenate(split(left), 1), weights, preferred_element_type=jnp.float32
        )
        mixed = (mixed[:, :GRP] + mixed[:, GRP:]).reshape(shape) * right
        sums = jnp.sum(mixed, axis=3, keepdims=True)
        total = total + jnp.sum(
            jnp.where(lane == spot + part * 32, sums, 0.0), axis=(0, 1)
        )
    return total


def whole_kernel(
    n_wide,
    n_narrow,
    n_blocks,
    groups_hbm,
    brick_hbm,
    freq_hbm,
    phase_hbm,
    blocks_hbm,
    core_hbm,
    ytab_hbm,
    xtab_hbm,
    out_ref,
    groups_ref,
    brick_ref,
    freq_ref,
    phase_ref,
    blocks_ref,
    core_ref,
    ytab_ref,
    xtab_ref,
    waves_ref,
    factor_ref,
    weight_ref,
    brick_col,
    piece_ref,
    place_send,
    place_recv,
    send_ref,
    recv_ref,
    core_part,
    core_pow,
    fold_ref,
    half_send,
    half_recv,
    acc_ref,
    load_sem,
    place_ssem,
    place_rsem,
    piece_ssem,
    piece_rsem,
    half_ssem,
    half_rsem,
):
    wide, narrow = lax.axis_index("wide"), lax.axis_index("narrow")
    loads = [
        pltpu.make_async_copy(src, dst, load_sem.at[i])
        for i, (src, dst) in enumerate(
            (
                (brick_hbm, brick_ref),
                (groups_hbm, groups_ref),
                (freq_hbm, freq_ref),
                (phase_hbm, phase_ref),
                (blocks_hbm, blocks_ref),
                (core_hbm, core_ref),
                (ytab_hbm, ytab_ref),
                (xtab_hbm, xtab_ref),
            )
        )
    ]
    for load in loads:
        load.start()

    barrier = pltpu.get_barrier_semaphore()

    def greet_wide(d, carry):
        peer = lax.rem(wide + d, n_wide)
        pl.semaphore_signal(
            barrier, inc=1, device_id=(peer, narrow), device_id_type=MESH
        )
        return carry

    def greet_narrow(d, carry):
        peer = lax.rem(narrow + d, n_narrow)
        pl.semaphore_signal(
            barrier, inc=1, device_id=(wide, peer), device_id_type=MESH
        )
        return carry

    lax.fori_loop(1, n_wide, greet_wide, 0)
    lax.fori_loop(1, n_narrow, greet_narrow, 0)

    loads[0].wait()
    loads[1].wait()
    brick_col[...] = jnp.zeros_like(brick_col)

    def spread(b, carry):
        brick_col[pl.ds(b, 1), :] = jnp.full((1, 128), brick_ref[b], jnp.int32)
        return carry

    lax.fori_loop(0, n_blocks, spread, 0)
    bricks = brick_col[...]
    row = lax.broadcasted_iota(jnp.int32, (128, 128), 0)
    lane = lax.broadcasted_iota(jnp.int32, (128, 128), 1)
    home = jnp.where(row < n_blocks, bricks >> 10, -1)
    home_t = jnp.transpose(home.astype(jnp.float32)).astype(jnp.int32)
    rank = jnp.sum(
        jnp.where((home == home_t) & (lane < row), 1.0, 0.0), axis=1, keepdims=True
    ).astype(jnp.int32)
    slot = jnp.where(row < n_blocks, 2 * home + rank, -1)
    slot_t = jnp.transpose(slot.astype(jnp.float32)).astype(jnp.int32)
    by = (bricks >> 5) & 31
    place = ((by >> 4) * 64 + (bricks & 3) * 16 + (by & 15) + 1).astype(jnp.bfloat16)
    slot_row = lax.broadcasted_iota(jnp.int32, (2 * n_wide, 128), 0)
    slot_row = jnp.where(slot_row < n_wide, 2 * slot_row, 2 * (slot_row - n_wide) + 1)
    pick = jnp.where(
        jnp.broadcast_to(slot_t[0:1], (2 * n_wide, 128)) == slot_row, 1.0, 0.0
    ).astype(jnp.bfloat16)[:, :32]
    first = lax.broadcasted_iota(jnp.int32, (32, 128), 1) < 64
    places = jnp.dot(pick, place[:32], preferred_element_type=jnp.float32) - 1.0
    place_send[:, 0, :] = jnp.where(first, places[:n_wide], places[n_wide:])
    pick = jnp.concatenate([pick, pick], 1)

    loads[2].wait()
    loads[3].wait()
    for g in range(waves_ref.shape[0]):
        at = slice(g * GRP, g * GRP + GRP)
        waves_ref[g, 0:3, :] = freq_ref[:, at]
        waves_ref[g, 3:6, :] = phase_ref[:, at]
        waves_ref[g, 6:8, :] = jnp.zeros((2, GRP), jnp.float32)
    loads[4].wait()
    piece_ref[...] = jnp.zeros_like(piece_ref)

    def prepare(b, carry):
        block_tables(
            b, groups_ref, brick_ref, waves_ref, blocks_ref, factor_ref, weight_ref
        )
        return carry

    lax.fori_loop(0, n_blocks, prepare, 0, unroll=4)

    def place_copy(d):
        peer = lax.rem(wide + d, n_wide)
        return pltpu.make_async_remote_copy(
            src_ref=place_send.at[peer],
            dst_ref=place_recv.at[wide],
            send_sem=place_ssem,
            recv_sem=place_rsem,
            device_id=(peer, narrow),
            device_id_type=MESH,
        )

    def piece_copy(h, d):
        peer = lax.rem(wide + d, n_wide)
        return pltpu.make_async_remote_copy(
            src_ref=send_ref.at[h, pl.ds(pl.multiple_of(peer * 8, 8), 8)],
            dst_ref=recv_ref.at[h, pl.ds(pl.multiple_of(wide * 8, 8), 8)],
            send_sem=piece_ssem.at[h],
            recv_sem=piece_rsem.at[h],
            device_id=(peer, narrow),
            device_id_type=MESH,
        )

    own8 = pl.ds(pl.multiple_of(wide * 8, 8), 8)
    for h in range(2):

        def work(b, carry, h=h):
            piece_ref[h, pl.ds(pl.multiple_of(b * 8, 8), 8), :] = half_piece(
                b, h, factor_ref, weight_ref
            )
            return carry

        lax.fori_loop(0, n_blocks, work, 0, unroll=8)
        for r in range(8):
            both = jnp.concatenate(split(piece_ref[h, pl.ds(r, 32, stride=8), :]), 0)
            slots = jnp.dot(pick, both, preferred_element_type=jnp.float32)
            send_ref[h, pl.ds(r, n_wide, stride=8), :] = jnp.where(
                first, slots[:n_wide], slots[n_wide:]
            )
        if h == 0:
            pl.semaphore_wait(barrier, n_wide + n_narrow - 2)

        def start_piece(d, carry, h=h):
            piece_copy(h, d).start()
            return carry

        lax.fori_loop(1, n_wide, start_piece, 0)
        recv_ref[h, own8] = send_ref[h, own8]
        if h == 0:

            def start_place(d, carry):
                place_copy(d).start()
                return carry

            lax.fori_loop(1, n_wide, start_place, 0)
            place_recv[wide] = place_send[wide]

    loads[5].wait()
    at = lax.broadcasted_iota(jnp.int32, (256, 256), 0)
    to = (
        ((at >> 4) & 1) * 128 + (at >> 7) * 64 + ((at >> 5) & 3) * 16 + (at & 15)
    )
    order = jnp.where(
        to == lax.broadcasted_iota(jnp.int32, (256, 256), 1), 1.0, 0.0
    ).astype(jnp.bfloat16)
    for r in range(4):
        rows = []
        for g in range(8):
            y = g % 4 * 8 + 2 * r + g // 4
            rows.append(
                jnp.concatenate(
                    [core_ref[pl.ds(y + t * 512, 16, stride=32), :] for t in range(2)],
                    1,
                )
            )
        value = jnp.concatenate(rows, 0)
        high, rest = value.astype(jnp.bfloat16), value
        rest = rest - high.astype(jnp.float32)
        moved = (
            jnp.dot(high, order, preferred_element_type=jnp.float32)
            + sum(
                jnp.dot(part, order, preferred_element_type=jnp.float32)
                for part in split(rest)
            )
        )
        for h in range(2):
            own = moved[:, h * 128 : h * 128 + 128]
            core_part[h, r * 128 : r * 128 + 128, :] = own
            core_pow[h, r * 128 : r * 128 + 128, :] = power43(own)

    wait_all(place_recv.at[pl.ds(0, n_wide - 1)], place_rsem)
    wait_all(place_send.at[pl.ds(0, n_wide - 1)], place_ssem)
    places = place_recv[:, 0, :]
    brick_lane = lax.broadcasted_iota(jnp.int32, (n_wide, 128), 1).astype(jnp.float32)
    spots = [
        jnp.where(places[:, k * 64 : k * 64 + 1] == brick_lane, 1.0, 0.0)
        for k in range(2)
    ]
    gather = jnp.transpose(jnp.concatenate([*spots, *spots], 0)).astype(jnp.bfloat16)

    chips = n_narrow // 2
    hops = [(2, 0), (2, 1), (1, 0), (3, 0), (1, 1), (3, 1), (0, 1), (0, 0)]

    def peer_at(hop):
        chip = lax.rem(narrow // 2 + hop[0], chips)
        return chip * 2 + lax.rem(narrow + hop[1], 2)

    def half_copy(h, i):
        peer = peer_at(hops[i])
        return pltpu.make_async_remote_copy(
            src_ref=half_send.at[h, peer],
            dst_ref=half_recv.at[h, narrow],
            send_sem=half_ssem.at[h, i],
            recv_sem=half_rsem.at[h, i],
            device_id=(wide, peer),
            device_id_type=MESH,
        )

    group = lax.broadcasted_iota(jnp.int32, (16, 128), 1) >> 4
    low16 = group < 4
    low64 = lax.broadcasted_iota(jnp.int32, (64, 128), 1) < 64
    for h in range(2):
        others = pl.ds(0, (n_wide - 1) * 8)
        wait_all(recv_ref.at[h, others], piece_rsem.at[h])
        wait_all(send_ref.at[h, others], piece_ssem.at[h])
        for r in range(4):
            even = recv_ref[h, pl.ds(2 * r, n_wide, stride=8), :]
            odd = recv_ref[h, pl.ds(2 * r + 1, n_wide, stride=8), :]
            got = jnp.concatenate(
                [
                    jnp.where(first, even, pltpu.roll(odd, 64, 1)),
                    jnp.where(first, pltpu.roll(even, 64, 1), odd),
                ],
                0,
            )
            sums = jnp.dot(
                gather,
                jnp.concatenate(split(got), 0),
                preferred_element_type=jnp.float32,
            )
            tiles = [sums[j * 16 : j * 16 + 16] for j in range(8)]
            for bit in (1, 2, 4):
                for j in range(8):
                    if not j & bit:
                        a, b = tiles[j], tiles[j | bit]
                        keep = (group & bit) == 0
                        tiles[j] = jnp.where(keep, a, pltpu.roll(b, 16 * bit, 1))
                        tiles[j | bit] = jnp.where(
                            keep, pltpu.roll(a, 128 - 16 * bit, 1), b
                        )
            for g in range(8):
                at = slice((r * 8 + g) * 16, (r * 8 + g) * 16 + 16)
                rho = core_part[h, at, :] + tiles[g]
                energy = energy_coef * (power43(jnp.abs(rho)) - core_pow[h, at, :])
                other = pltpu.roll(energy, 64, 1)
                fold = jnp.where(low16, energy + other, other - energy)
                high = fold.astype(jnp.bfloat16).astype(jnp.float32)
                rest = fold - high
                fold_ref[h, 0, at, :] = jnp.where(
                    low16, high, pltpu.roll(rest, 64, 1)
                ).astype(jnp.bfloat16)
                fold_ref[h, 1, at, :] = jnp.where(
                    low16, pltpu.roll(high, 64, 1), rest
                ).astype(jnp.bfloat16)
        if h == 0:
            loads[6].wait()
        for i, hop in enumerate(hops):
            peer = peer_at(hop)
            target = half_recv.at[h, narrow] if hop == (0, 0) else half_send.at[h, peer]
            for parity in range(2):
                half = jnp.dot(
                    ytab_ref[0, peer, parity],
                    fold_ref[h, parity],
                    preferred_element_type=jnp.float32,
                ) + jnp.dot(
                    ytab_ref[1, peer, parity],
                    fold_ref[h, parity],
                    preferred_element_type=jnp.float32,
                )
                half = half + pltpu.roll(half, 64, 1)
                target[pl.ds(parity, 64, stride=2), :] = jnp.where(
                    low64, half[:64], half[64:]
                )
            if hop != (0, 0):
                half_copy(h, i).start()

    loads[7].wait()
    low256 = (lax.broadcasted_iota(jnp.int32, (128, 256), 1) & 127) < 64
    waits = {0: (6,), 1: (3, 5), 3: (2, 4), 2: (0, 1)}
    for h in range(2):
        for on, copies in waits.items():
            for i in copies:
                half_copy(h, i).wait_recv()
            chip = lax.rem(narrow // 2 + on, chips)
            ours = [half_recv[h, 2 * chip + core] for core in range(2)]
            turned = [pltpu.roll(own, 64, 1) for own in ours]
            real, imag = jnp.concatenate(ours, 1), jnp.concatenate(turned, 1)
            high, low = split(
                jnp.concatenate([real, jnp.where(low256, imag, -imag)], 0)
            )
            part = (
                jnp.dot(high, xtab_ref[0, h, chip], preferred_element_type=jnp.float32)
                + jnp.dot(low, xtab_ref[0, h, chip], preferred_element_type=jnp.float32)
                + jnp.dot(high, xtab_ref[1, h, chip], preferred_element_type=jnp.float32)
            )
            if (h, on) == (0, 0):
                acc_ref[...] = part
            elif (h, on) != (1, 2):
                acc_ref[...] += part
            else:
                total = acc_ref[...] + part
                for c in range(2):
                    out_ref[0, c] = total[c * 128 : c * 128 + 128]

    for h in range(2):
        for i in range(len(hops) - 1):
            half_copy(h, i).wait_send()


def local(density_blocks, block_groups, block_brick, orbital_freq, orbital_phase, core_density):
    n_wide, n_narrow = lax.axis_size("wide"), lax.axis_size("narrow")
    n_blocks = density_blocks.shape[0]
    ytab, xtab = y_tables(n_narrow), x_tables(n_narrow // 2)
    vmem = pl.BlockSpec(memory_space=pltpu.VMEM)
    hbm = pl.BlockSpec(memory_space=pltpu.HBM)
    f32, bf16 = jnp.float32, jnp.bfloat16
    rows = NY // n_narrow
    return pl.pallas_call(
        functools.partial(whole_kernel, n_wide, n_narrow, n_blocks),
        out_shape=jax.ShapeDtypeStruct((1, 2, rows, NX // 2), f32),
        in_specs=[hbm] * 8,
        out_specs=vmem,
        scratch_shapes=[
            pltpu.SMEM((2, n_blocks), jnp.int32),
            pltpu.SMEM((n_blocks,), jnp.int32),
            pltpu.VMEM(orbital_freq.shape, f32),
            pltpu.VMEM(orbital_phase.shape, f32),
            pltpu.VMEM(density_blocks.shape, f32),
            pltpu.VMEM(core_density.shape[1:], f32),
            pltpu.VMEM(ytab.shape, bf16),
            pltpu.VMEM(xtab.shape, bf16),
            pltpu.VMEM((orbital_freq.shape[1] // GRP, 8, GRP), f32),
            pltpu.VMEM((n_blocks, 4, 32, GRP), f32),
            pltpu.VMEM((n_blocks, 2 * GRP, 2 * GRP), bf16),
            pltpu.VMEM((128, 128), jnp.int32),
            pltpu.VMEM((2, 32 * 8, 128), f32),
            pltpu.VMEM((n_wide, 1, 128), f32),
            pltpu.VMEM((n_wide, 1, 128), f32),
            pltpu.VMEM((2, n_wide * 8, 128), f32),
            pltpu.VMEM((2, n_wide * 8, 128), f32),
            pltpu.VMEM((2, NY // 2, 128), f32),
            pltpu.VMEM((2, NY // 2, 128), f32),
            pltpu.VMEM((2, 2, NY // 2, 128), bf16),
            pltpu.VMEM((2, n_narrow, 128, 128), f32),
            pltpu.VMEM((2, n_narrow, 128, 128), f32),
            pltpu.VMEM((256, NX // 2), f32),
            pltpu.SemaphoreType.DMA((8,)),
            pltpu.SemaphoreType.DMA,
            pltpu.SemaphoreType.DMA,
            pltpu.SemaphoreType.DMA((2,)),
            pltpu.SemaphoreType.DMA((2,)),
            pltpu.SemaphoreType.DMA((2, n_narrow)),
            pltpu.SemaphoreType.DMA((2, n_narrow)),
        ],
        compiler_params=pltpu.CompilerParams(
            collective_id=0, has_side_effects=True, vmem_limit_bytes=48 * 2**20
        ),
    )(
        *(
            pltpu.with_memory_space_constraint(array, pltpu.HBM)
            for array in (
                block_groups.T,
                block_brick,
                orbital_freq,
                orbital_phase,
                density_blocks,
                core_density.reshape(core_density.shape[1:]),
                jnp.asarray(ytab),
                jnp.asarray(xtab),
            )
        ),
    )


def solution(mesh):
    return jax.shard_map(
        local,
        mesh=mesh,
        in_specs=(
            P(("wide", "narrow"), None, None),
            P(("wide", "narrow"), None),
            P(("wide", "narrow")),
            P(),
            P(),
            P("wide", None, "narrow"),
        ),
        out_specs=P("wide", None, "narrow", None),
        check_vma=False,
    )
```

```python
import functools
import math

import jax
import jax.numpy as jnp
import ml_dtypes
import numpy as np
from jax import lax
from jax.experimental import pallas as pl
from jax.experimental.pallas import tpu as pltpu
from jax.sharding import PartitionSpec as P

NX = 1024
NY = 1024
GRP = 128
BY = 32
BX = 32
MESH = pl.DeviceIdType.MESH

energy_coef = -0.75 * (3.0 / math.pi) ** (1.0 / 3.0)

INV_TURN = 1.0 / (2.0 * math.pi)
PI_HI = 3.140625
PI_LO = math.pi - PI_HI
SINE = (
    2.604579135698264e-06,
    -0.00019808792785020506,
    0.008333047269825162,
    -0.16666657833027024,
    0.9999999956345141,
)


def cosine(angle):
    turns = jnp.round(angle * INV_TURN)
    half = (0.5 * angle - turns * PI_HI) - turns * PI_LO
    square = half * half
    poly = SINE[0]
    for coef in SINE[1:]:
        poly = poly * square + coef
    sine = half * poly
    return 1.0 - 2.0 * (sine * sine)


def split(value):
    high = value.astype(jnp.bfloat16)
    return high, (value - high.astype(jnp.float32)).astype(jnp.bfloat16)


def power43(value):
    return jnp.exp(jnp.log(value) * (4.0 / 3.0))


def split_table(table):
    table = np.asarray(table, np.float32)
    high = table.astype(ml_dtypes.bfloat16)
    low = (table - high.astype(np.float32)).astype(ml_dtypes.bfloat16)
    return np.stack([high, low])


def y_tables(parts):
    rows = NY // parts
    col = np.arange(NY // 2)
    r, g = col // 128, col // 16 % 8
    y = col % 16 * 32 + g % 4 * 8 + 2 * r + g // 4
    ky = (
        np.arange(parts)[:, None, None] * rows
        + np.arange(2)[None, :, None]
        + 2 * np.arange(rows // 2)[None, None, :]
    )
    angle = 2.0 * np.pi / NY * (ky[..., None] * y % NY)
    return split_table(
        np.concatenate([np.cos(angle), -np.sin(angle)], 2) / math.sqrt(NY)
    )


def x_tables(chips):
    h, chip, core, xb, xi = np.ix_(*map(np.arange, (2, chips, 2, 4, 16)))
    x = (chip * 2 + core) * 128 + xb * 32 + h * 16 + xi
    x = x.reshape(2, chips, 2, 64, 1)
    angle = 2.0 * np.pi / NX * (x * np.arange(NX // 2) % NX)
    both = np.stack([np.cos(angle), np.sin(angle)], 3) / math.sqrt(NX)
    return split_table(both.reshape(2, chips, 256, NX // 2))


def wait_all(ref, sem):
    pltpu.make_async_copy(ref, ref, sem).wait()


def block_factors(b, groups_ref, brick_ref, waves_ref, factor_ref):
    brick = brick_ref[b]
    x0 = ((brick & 31) * BX).astype(jnp.float32)
    y0 = (((brick >> 5) & 31) * BY).astype(jnp.float32)
    z0 = (brick >> 10).astype(jnp.float32)
    step = lax.broadcasted_iota(jnp.int32, (32, GRP), 0).astype(jnp.float32)
    xs, ys = step + x0, step + y0
    for side in range(2):
        wave = waves_ref[groups_ref[side, b]]
        along_z = cosine(z0 * wave[2:3] + wave[5:6])
        factor_ref[b, 2 * side] = cosine(xs * wave[0:1] + wave[3:4]) * along_z
        factor_ref[b, 2 * side + 1] = cosine(ys * wave[1:2] + wave[4:5])


def block_halves(b, blocks_ref, weight_ref):
    high, low = split(blocks_ref[b])
    weight_ref[b] = jnp.concatenate(
        [
            jnp.concatenate([high, low], 1),
            jnp.concatenate([high, jnp.zeros_like(low)], 1),
        ],
        0,
    )


def half_piece(b, h, factor_ref, weight_ref):
    cols = slice(h * 16, h * 16 + 16)
    left_x, right_x = factor_ref[b, 0, cols], factor_ref[b, 2, cols]
    weights = weight_ref[b]
    shape = (2, 16, 8, GRP)
    lane = lax.broadcasted_iota(jnp.int32, shape, 3) & 63
    spot = lax.broadcasted_iota(jnp.int32, shape, 1) + 16 * lax.broadcasted_iota(
        jnp.int32, shape, 0
    )
    total = jnp.zeros((8, 128), jnp.float32)
    for part in range(2):
        rows = slice(part * 16, part * 16 + 16)
        left_y = factor_ref[b, 1, rows].reshape(2, 1, 8, GRP)
        right_y = factor_ref[b, 3, rows].reshape(2, 1, 8, GRP)
        left = (left_x[None, :, None, :] * left_y).reshape(256, GRP)
        right = right_x[None, :, None, :] * right_y
        mixed = jnp.dot(
            jnp.concatenate(split(left), 1), weights, preferred_element_type=jnp.float32
        )
        mixed = (mixed[:, :GRP] + mixed[:, GRP:]).reshape(shape) * right
        sums = jnp.sum(mixed, axis=3, keepdims=True)
        total = total + jnp.sum(
            jnp.where(lane == spot + part * 32, sums, 0.0), axis=(0, 1)
        )
    return total


def whole_kernel(
    n_wide,
    n_narrow,
    n_blocks,
    groups_hbm,
    brick_hbm,
    freq_hbm,
    phase_hbm,
    blocks_hbm,
    core_hbm,
    ytab_hbm,
    xtab_hbm,
    out_ref,
    groups_ref,
    brick_ref,
    freq_ref,
    phase_ref,
    blocks_ref,
    core_ref,
    ytab_ref,
    xtab_ref,
    waves_ref,
    factor_ref,
    weight_ref,
    brick_col,
    piece_ref,
    place_send,
    place_recv,
    send_ref,
    recv_ref,
    core_part,
    core_pow,
    fold_ref,
    half_send,
    half_recv,
    acc_ref,
    load_sem,
    place_ssem,
    place_rsem,
    piece_ssem,
    piece_rsem,
    half_ssem,
    half_rsem,
):
    wide, narrow = lax.axis_index("wide"), lax.axis_index("narrow")
    loads = [
        pltpu.make_async_copy(src, dst, load_sem.at[i])
        for i, (src, dst) in enumerate(
            (
                (brick_hbm, brick_ref),
                (groups_hbm, groups_ref),
                (freq_hbm, freq_ref),
                (phase_hbm, phase_ref),
                (blocks_hbm, blocks_ref),
                (core_hbm, core_ref),
                (ytab_hbm, ytab_ref),
                (xtab_hbm, xtab_ref),
            )
        )
    ]
    for load in loads[:5]:
        load.start()

    barrier = pltpu.get_barrier_semaphore()

    def greet_wide(d, carry):
        peer = lax.rem(wide + d, n_wide)
        pl.semaphore_signal(
            barrier, inc=1, device_id=(peer, narrow), device_id_type=MESH
        )
        return carry

    def greet_narrow(d, carry):
        peer = lax.rem(narrow + d, n_narrow)
        pl.semaphore_signal(
            barrier, inc=1, device_id=(wide, peer), device_id_type=MESH
        )
        return carry

    lax.fori_loop(1, n_wide, greet_wide, 0)
    lax.fori_loop(1, n_narrow, greet_narrow, 0)

    loads[0].wait()
    loads[1].wait()
    brick_col[...] = jnp.zeros_like(brick_col)

    def spread(b, carry):
        brick_col[pl.ds(b, 1), :] = jnp.full((1, 128), brick_ref[b], jnp.int32)
        return carry

    lax.fori_loop(0, n_blocks, spread, 0)
    bricks = brick_col[...]
    row = lax.broadcasted_iota(jnp.int32, (128, 128), 0)
    lane = lax.broadcasted_iota(jnp.int32, (128, 128), 1)
    home = jnp.where(row < n_blocks, bricks >> 10, -1)
    home_t = jnp.transpose(home.astype(jnp.float32)).astype(jnp.int32)
    rank = jnp.sum(
        jnp.where((home == home_t) & (lane < row), 1.0, 0.0), axis=1, keepdims=True
    ).astype(jnp.int32)
    slot = jnp.where(row < n_blocks, 2 * home + rank, -1)
    slot_t = jnp.transpose(slot.astype(jnp.float32)).astype(jnp.int32)
    by = (bricks >> 5) & 31
    place = ((by >> 4) * 64 + (bricks & 3) * 16 + (by & 15) + 1).astype(jnp.bfloat16)
    slot_row = lax.broadcasted_iota(jnp.int32, (2 * n_wide, 128), 0)
    slot_row = jnp.where(slot_row < n_wide, 2 * slot_row, 2 * (slot_row - n_wide) + 1)
    pick = jnp.where(
        jnp.broadcast_to(slot_t[0:1], (2 * n_wide, 128)) == slot_row, 1.0, 0.0
    ).astype(jnp.bfloat16)[:, :32]
    first = lax.broadcasted_iota(jnp.int32, (32, 128), 1) < 64
    places = jnp.dot(pick, place[:32], preferred_element_type=jnp.float32) - 1.0
    place_send[:, 0, :] = jnp.where(first, places[:n_wide], places[n_wide:])
    pick = jnp.concatenate([pick, pick], 1)

    loads[2].wait()
    loads[3].wait()
    for g in range(waves_ref.shape[0]):
        at = slice(g * GRP, g * GRP + GRP)
        waves_ref[g, 0:3, :] = freq_ref[:, at]
        waves_ref[g, 3:6, :] = phase_ref[:, at]
        waves_ref[g, 6:8, :] = jnp.zeros((2, GRP), jnp.float32)
    piece_ref[...] = jnp.zeros_like(piece_ref)

    def prepare(b, carry):
        block_factors(b, groups_ref, brick_ref, waves_ref, factor_ref)
        return carry

    lax.fori_loop(0, n_blocks, prepare, 0, unroll=4)
    loads[4].wait()
    for load in loads[5:]:
        load.start()

    def halve(b, carry):
        block_halves(b, blocks_ref, weight_ref)
        return carry

    lax.fori_loop(0, n_blocks, halve, 0, unroll=4)

    def place_copy(d):
        peer = lax.rem(wide + d, n_wide)
        return pltpu.make_async_remote_copy(
            src_ref=place_send.at[peer],
            dst_ref=place_recv.at[wide],
            send_sem=place_ssem,
            recv_sem=place_rsem,
            device_id=(peer, narrow),
            device_id_type=MESH,
        )

    def piece_copy(h, d):
        peer = lax.rem(wide + d, n_wide)
        return pltpu.make_async_remote_copy(
            src_ref=send_ref.at[h, pl.ds(pl.multiple_of(peer * 8, 8), 8)],
            dst_ref=recv_ref.at[h, pl.ds(pl.multiple_of(wide * 8, 8), 8)],
            send_sem=piece_ssem.at[h],
            recv_sem=piece_rsem.at[h],
            device_id=(peer, narrow),
            device_id_type=MESH,
        )

    own8 = pl.ds(pl.multiple_of(wide * 8, 8), 8)

    def compute_half(h):
        def work(b, carry):
            piece_ref[h, pl.ds(pl.multiple_of(b * 8, 8), 8), :] = half_piece(
                b, h, factor_ref, weight_ref
            )
            return carry

        lax.fori_loop(0, n_blocks, work, 0, unroll=8)
        for r in range(8):
            both = jnp.concatenate(split(piece_ref[h, pl.ds(r, 32, stride=8), :]), 0)
            slots = jnp.dot(pick, both, preferred_element_type=jnp.float32)
            send_ref[h, pl.ds(r, n_wide, stride=8), :] = jnp.where(
                first, slots[:n_wide], slots[n_wide:]
            )

    def send_half(h):
        def start_piece(d, carry):
            piece_copy(h, d).start()
            return carry

        lax.fori_loop(1, n_wide, start_piece, 0)
        recv_ref[h, own8] = send_ref[h, own8]

    compute_half(0)
    pl.semaphore_wait(barrier, n_wide + n_narrow - 2)
    send_half(0)

    def start_place(d, carry):
        place_copy(d).start()
        return carry

    lax.fori_loop(1, n_wide, start_place, 0)
    place_recv[wide] = place_send[wide]

    loads[5].wait()
    at = lax.broadcasted_iota(jnp.int32, (256, 256), 0)
    to = (
        ((at >> 4) & 1) * 128 + (at >> 7) * 64 + ((at >> 5) & 3) * 16 + (at & 15)
    )
    order = jnp.where(
        to == lax.broadcasted_iota(jnp.int32, (256, 256), 1), 1.0, 0.0
    ).astype(jnp.bfloat16)
    for r in range(4):
        rows = []
        for g in range(8):
            y = g % 4 * 8 + 2 * r + g // 4
            rows.append(
                jnp.concatenate(
                    [core_ref[pl.ds(y + t * 512, 16, stride=32), :] for t in range(2)],
                    1,
                )
            )
        value = jnp.concatenate(rows, 0)
        high, rest = value.astype(jnp.bfloat16), value
        rest = rest - high.astype(jnp.float32)
        moved = (
            jnp.dot(high, order, preferred_element_type=jnp.float32)
            + sum(
                jnp.dot(part, order, preferred_element_type=jnp.float32)
                for part in split(rest)
            )
        )
        for h in range(2):
            own = moved[:, h * 128 : h * 128 + 128]
            core_part[h, r * 128 : r * 128 + 128, :] = own
            core_pow[h, r * 128 : r * 128 + 128, :] = power43(own)

    compute_half(1)
    send_half(1)
    wait_all(place_recv.at[pl.ds(0, n_wide - 1)], place_rsem)
    wait_all(place_send.at[pl.ds(0, n_wide - 1)], place_ssem)
    places = place_recv[:, 0, :]
    brick_lane = lax.broadcasted_iota(jnp.int32, (n_wide, 128), 1).astype(jnp.float32)
    spots = [
        jnp.where(places[:, k * 64 : k * 64 + 1] == brick_lane, 1.0, 0.0)
        for k in range(2)
    ]
    gather = jnp.transpose(jnp.concatenate([*spots, *spots], 0)).astype(jnp.bfloat16)

    chips = n_narrow // 2
    hops = [(1, 0), (3, 0), (1, 1), (3, 1), (2, 0), (2, 1), (0, 1), (0, 0)]

    def peer_at(hop):
        chip = lax.rem(narrow // 2 + hop[0], chips)
        return chip * 2 + lax.rem(narrow + hop[1], 2)

    def half_copy(h, i):
        peer = peer_at(hops[i])
        return pltpu.make_async_remote_copy(
            src_ref=half_send.at[h, peer],
            dst_ref=half_recv.at[h, narrow],
            send_sem=half_ssem.at[h, i],
            recv_sem=half_rsem.at[h, i],
            device_id=(wide, peer),
            device_id_type=MESH,
        )

    group = lax.broadcasted_iota(jnp.int32, (16, 128), 1) >> 4
    low16 = group < 4
    low64 = lax.broadcasted_iota(jnp.int32, (64, 128), 1) < 64
    for h in range(2):
        others = pl.ds(0, (n_wide - 1) * 8)
        wait_all(recv_ref.at[h, others], piece_rsem.at[h])
        wait_all(send_ref.at[h, others], piece_ssem.at[h])
        for r in range(4):
            even = recv_ref[h, pl.ds(2 * r, n_wide, stride=8), :]
            odd = recv_ref[h, pl.ds(2 * r + 1, n_wide, stride=8), :]
            got = jnp.concatenate(
                [
                    jnp.where(first, even, pltpu.roll(odd, 64, 1)),
                    jnp.where(first, pltpu.roll(even, 64, 1), odd),
                ],
                0,
            )
            sums = jnp.dot(
                gather,
                jnp.concatenate(split(got), 0),
                preferred_element_type=jnp.float32,
            )
            tiles = [sums[j * 16 : j * 16 + 16] for j in range(8)]
            for bit in (1, 2, 4):
                for j in range(8):
                    if not j & bit:
                        a, b = tiles[j], tiles[j | bit]
                        keep = (group & bit) == 0
                        tiles[j] = jnp.where(keep, a, pltpu.roll(b, 16 * bit, 1))
                        tiles[j | bit] = jnp.where(
                            keep, pltpu.roll(a, 128 - 16 * bit, 1), b
                        )
            for g in range(8):
                at = slice((r * 8 + g) * 16, (r * 8 + g) * 16 + 16)
                rho = core_part[h, at, :] + tiles[g]
                energy = energy_coef * (power43(jnp.abs(rho)) - core_pow[h, at, :])
                other = pltpu.roll(energy, 64, 1)
                fold = jnp.where(low16, energy + other, other - energy)
                high = fold.astype(jnp.bfloat16).astype(jnp.float32)
                rest = fold - high
                fold_ref[h, 0, at, :] = jnp.where(
                    low16, high, pltpu.roll(rest, 64, 1)
                ).astype(jnp.bfloat16)
                fold_ref[h, 1, at, :] = jnp.where(
                    low16, pltpu.roll(high, 64, 1), rest
                ).astype(jnp.bfloat16)
        if h == 0:
            loads[6].wait()
        for i, hop in enumerate(hops):
            peer = peer_at(hop)
            target = half_recv.at[h, narrow] if hop == (0, 0) else half_send.at[h, peer]
            for parity in range(2):
                half = jnp.dot(
                    ytab_ref[0, peer, parity],
                    fold_ref[h, parity],
                    preferred_element_type=jnp.float32,
                ) + jnp.dot(
                    ytab_ref[1, peer, parity],
                    fold_ref[h, parity],
                    preferred_element_type=jnp.float32,
                )
                half = half + pltpu.roll(half, 64, 1)
                target[pl.ds(parity, 64, stride=2), :] = jnp.where(
                    low64, half[:64], half[64:]
                )
            if hop != (0, 0):
                half_copy(h, i).start()

    loads[7].wait()
    low256 = (lax.broadcasted_iota(jnp.int32, (128, 256), 1) & 127) < 64
    waits = {0: (6,), 1: (1, 3), 3: (0, 2), 2: (4, 5)}
    for h in range(2):
        for on, copies in waits.items():
            for i in copies:
                half_copy(h, i).wait_recv()
            chip = lax.rem(narrow // 2 + on, chips)
            ours = [half_recv[h, 2 * chip + core] for core in range(2)]
            turned = [pltpu.roll(own, 64, 1) for own in ours]
            real, imag = jnp.concatenate(ours, 1), jnp.concatenate(turned, 1)
            high, low = split(
                jnp.concatenate([real, jnp.where(low256, imag, -imag)], 0)
            )
            part = (
                jnp.dot(high, xtab_ref[0, h, chip], preferred_element_type=jnp.float32)
                + jnp.dot(low, xtab_ref[0, h, chip], preferred_element_type=jnp.float32)
                + jnp.dot(high, xtab_ref[1, h, chip], preferred_element_type=jnp.float32)
            )
            if (h, on) == (0, 0):
                acc_ref[...] = part
            elif (h, on) != (1, 2):
                acc_ref[...] += part
            else:
                total = acc_ref[...] + part
                for c in range(2):
                    out_ref[0, c] = total[c * 128 : c * 128 + 128]

    for h in range(2):
        for i in range(len(hops) - 1):
            half_copy(h, i).wait_send()


def local(density_blocks, block_groups, block_brick, orbital_freq, orbital_phase, core_density):
    n_wide, n_narrow = lax.axis_size("wide"), lax.axis_size("narrow")
    n_blocks = density_blocks.shape[0]
    ytab, xtab = y_tables(n_narrow), x_tables(n_narrow // 2)
    vmem = pl.BlockSpec(memory_space=pltpu.VMEM)
    hbm = pl.BlockSpec(memory_space=pltpu.HBM)
    f32, bf16 = jnp.float32, jnp.bfloat16
    rows = NY // n_narrow
    return pl.pallas_call(
        functools.partial(whole_kernel, n_wide, n_narrow, n_blocks),
        out_shape=jax.ShapeDtypeStruct((1, 2, rows, NX // 2), f32),
        in_specs=[hbm] * 8,
        out_specs=vmem,
        scratch_shapes=[
            pltpu.SMEM((2, n_blocks), jnp.int32),
            pltpu.SMEM((n_blocks,), jnp.int32),
            pltpu.VMEM(orbital_freq.shape, f32),
            pltpu.VMEM(orbital_phase.shape, f32),
            pltpu.VMEM(density_blocks.shape, f32),
            pltpu.VMEM(core_density.shape[1:], f32),
            pltpu.VMEM(ytab.shape, bf16),
            pltpu.VMEM(xtab.shape, bf16),
            pltpu.VMEM((orbital_freq.shape[1] // GRP, 8, GRP), f32),
            pltpu.VMEM((n_blocks, 4, 32, GRP), f32),
            pltpu.VMEM((n_blocks, 2 * GRP, 2 * GRP), bf16),
            pltpu.VMEM((128, 128), jnp.int32),
            pltpu.VMEM((2, 32 * 8, 128), f32),
            pltpu.VMEM((n_wide, 1, 128), f32),
            pltpu.VMEM((n_wide, 1, 128), f32),
            pltpu.VMEM((2, n_wide * 8, 128), f32),
            pltpu.VMEM((2, n_wide * 8, 128), f32),
            pltpu.VMEM((2, NY // 2, 128), f32),
            pltpu.VMEM((2, NY // 2, 128), f32),
            pltpu.VMEM((2, 2, NY // 2, 128), bf16),
            pltpu.VMEM((2, n_narrow, 128, 128), f32),
            pltpu.VMEM((2, n_narrow, 128, 128), f32),
            pltpu.VMEM((256, NX // 2), f32),
            pltpu.SemaphoreType.DMA((8,)),
            pltpu.SemaphoreType.DMA,
            pltpu.SemaphoreType.DMA,
            pltpu.SemaphoreType.DMA((2,)),
            pltpu.SemaphoreType.DMA((2,)),
            pltpu.SemaphoreType.DMA((2, n_narrow)),
            pltpu.SemaphoreType.DMA((2, n_narrow)),
        ],
        compiler_params=pltpu.CompilerParams(
            collective_id=0, has_side_effects=True, vmem_limit_bytes=48 * 2**20
        ),
    )(
        *(
            pltpu.with_memory_space_constraint(array, pltpu.HBM)
            for array in (
                block_groups.T,
                block_brick,
                orbital_freq,
                orbital_phase,
                density_blocks,
                core_density.reshape(core_density.shape[1:]),
                jnp.asarray(ytab),
                jnp.asarray(xtab),
            )
        ),
    )


def solution(mesh):
    return jax.shard_map(
        local,
        mesh=mesh,
        in_specs=(
            P(("wide", "narrow"), None, None),
            P(("wide", "narrow"), None),
            P(("wide", "narrow")),
            P(),
            P(),
            P("wide", None, "narrow"),
        ),
        out_specs=P("wide", None, "narrow", None),
        check_vma=False,
    )
```

```python
import functools
import math

import jax
import jax.numpy as jnp
import ml_dtypes
import numpy as np
from jax import lax
from jax.experimental import pallas as pl
from jax.experimental.pallas import tpu as pltpu
from jax.sharding import PartitionSpec as P

NX = 1024
NY = 1024
GRP = 128
BY = 32
BX = 32
MESH = pl.DeviceIdType.MESH

energy_coef = -0.75 * (3.0 / math.pi) ** (1.0 / 3.0)

INV_TURN = 1.0 / (2.0 * math.pi)
PI_HI = 3.140625
PI_LO = math.pi - PI_HI
SINE = (
    2.604579135698264e-06,
    -0.00019808792785020506,
    0.008333047269825162,
    -0.16666657833027024,
    0.9999999956345141,
)


def cosine(angle):
    turns = jnp.round(angle * INV_TURN)
    half = (0.5 * angle - turns * PI_HI) - turns * PI_LO
    square = half * half
    poly = SINE[0]
    for coef in SINE[1:]:
        poly = poly * square + coef
    sine = half * poly
    return 1.0 - 2.0 * (sine * sine)


def split(value):
    high = value.astype(jnp.bfloat16)
    return high, (value - high.astype(jnp.float32)).astype(jnp.bfloat16)


def power43(value):
    return jnp.exp(jnp.log(value) * (4.0 / 3.0))


def split_table(table):
    table = np.asarray(table, np.float32)
    high = table.astype(ml_dtypes.bfloat16)
    low = (table - high.astype(np.float32)).astype(ml_dtypes.bfloat16)
    return np.stack([high, low])


def y_tables(parts):
    rows = NY // parts
    col = np.arange(NY // 2)
    r, g = col // 128, col // 16 % 8
    y = col % 16 * 32 + g % 4 * 8 + 2 * r + g // 4
    ky = (
        np.arange(parts)[:, None, None] * rows
        + np.arange(2)[None, :, None]
        + 2 * np.arange(rows // 2)[None, None, :]
    )
    angle = 2.0 * np.pi / NY * (ky[..., None] * y % NY)
    return split_table(
        np.concatenate([np.cos(angle), -np.sin(angle)], 2) / math.sqrt(NY)
    )


def x_tables(chips):
    h, chip, core, xb, xi = np.ix_(*map(np.arange, (2, chips, 2, 4, 16)))
    x = (chip * 2 + core) * 128 + xb * 32 + h * 16 + xi
    x = x.reshape(2, chips, 2, 64, 1)
    angle = 2.0 * np.pi / NX * (x * np.arange(NX // 2) % NX)
    both = np.stack([np.cos(angle), np.sin(angle)], 3) / math.sqrt(NX)
    return split_table(both.reshape(2, chips, 256, NX // 2))


def wait_all(ref, sem):
    pltpu.make_async_copy(ref, ref, sem).wait()


def block_factors(b, groups_ref, brick_ref, waves_ref, factor_ref):
    brick = brick_ref[b]
    x0 = ((brick & 31) * BX).astype(jnp.float32)
    y0 = (((brick >> 5) & 31) * BY).astype(jnp.float32)
    z0 = (brick >> 10).astype(jnp.float32)
    step = lax.broadcasted_iota(jnp.int32, (32, GRP), 0).astype(jnp.float32)
    xs, ys = step + x0, step + y0
    for side in range(2):
        wave = waves_ref[groups_ref[side, b]]
        along_z = cosine(z0 * wave[2:3] + wave[5:6])
        factor_ref[b, 2 * side] = cosine(xs * wave[0:1] + wave[3:4]) * along_z
        factor_ref[b, 2 * side + 1] = cosine(ys * wave[1:2] + wave[4:5])


def block_halves(b, blocks_ref, weight_ref):
    high, low = split(blocks_ref[b])
    weight_ref[b] = jnp.concatenate(
        [
            jnp.concatenate([high, low], 1),
            jnp.concatenate([high, jnp.zeros_like(low)], 1),
        ],
        0,
    )


def half_piece(b, h, factor_ref, weight_ref):
    cols = slice(h * 16, h * 16 + 16)
    left_x, right_x = factor_ref[b, 0, cols], factor_ref[b, 2, cols]
    weights = weight_ref[b]
    shape = (2, 16, 8, GRP)
    lane = lax.broadcasted_iota(jnp.int32, shape, 3) & 63
    spot = lax.broadcasted_iota(jnp.int32, shape, 1) + 16 * lax.broadcasted_iota(
        jnp.int32, shape, 0
    )
    total = jnp.zeros((8, 128), jnp.float32)
    for part in range(2):
        rows = slice(part * 16, part * 16 + 16)
        left_y = factor_ref[b, 1, rows].reshape(2, 1, 8, GRP)
        right_y = factor_ref[b, 3, rows].reshape(2, 1, 8, GRP)
        left = (left_x[None, :, None, :] * left_y).reshape(256, GRP)
        right = right_x[None, :, None, :] * right_y
        mixed = jnp.dot(
            jnp.concatenate(split(left), 1), weights, preferred_element_type=jnp.float32
        )
        mixed = (mixed[:, :GRP] + mixed[:, GRP:]).reshape(shape) * right
        sums = jnp.sum(mixed, axis=3, keepdims=True)
        total = total + jnp.sum(
            jnp.where(lane == spot + part * 32, sums, 0.0), axis=(0, 1)
        )
    return total


def whole_kernel(
    n_wide,
    n_narrow,
    n_blocks,
    groups_hbm,
    brick_hbm,
    freq_hbm,
    phase_hbm,
    blocks_hbm,
    core_hbm,
    ytab_hbm,
    xtab_hbm,
    out_ref,
    groups_ref,
    brick_ref,
    freq_ref,
    phase_ref,
    blocks_ref,
    core_ref,
    ytab_ref,
    xtab_ref,
    waves_ref,
    factor_ref,
    weight_ref,
    brick_col,
    piece_ref,
    place_send,
    place_recv,
    send_ref,
    recv_ref,
    core_part,
    core_pow,
    fold_ref,
    half_send,
    half_recv,
    acc_ref,
    load_sem,
    place_ssem,
    place_rsem,
    piece_ssem,
    piece_rsem,
    half_ssem,
    half_rsem,
):
    wide, narrow = lax.axis_index("wide"), lax.axis_index("narrow")
    loads = [
        pltpu.make_async_copy(src, dst, load_sem.at[i])
        for i, (src, dst) in enumerate(
            (
                (brick_hbm, brick_ref),
                (groups_hbm, groups_ref),
                (freq_hbm, freq_ref),
                (phase_hbm, phase_ref),
                (blocks_hbm, blocks_ref),
                (core_hbm, core_ref),
                (ytab_hbm, ytab_ref),
                (xtab_hbm, xtab_ref),
            )
        )
    ]
    for load in loads[:5]:
        load.start()

    barrier = pltpu.get_barrier_semaphore()

    def greet_wide(d, carry):
        peer = lax.rem(wide + d, n_wide)
        pl.semaphore_signal(
            barrier, inc=1, device_id=(peer, narrow), device_id_type=MESH
        )
        return carry

    def greet_narrow(d, carry):
        peer = lax.rem(narrow + d, n_narrow)
        pl.semaphore_signal(
            barrier, inc=1, device_id=(wide, peer), device_id_type=MESH
        )
        return carry

    lax.fori_loop(1, n_wide, greet_wide, 0)
    lax.fori_loop(1, n_narrow, greet_narrow, 0)

    loads[0].wait()
    loads[1].wait()
    brick_col[...] = jnp.zeros_like(brick_col)

    def spread(b, carry):
        brick_col[pl.ds(b, 1), :] = jnp.full((1, 128), brick_ref[b], jnp.int32)
        return carry

    lax.fori_loop(0, n_blocks, spread, 0)
    bricks = brick_col[...]
    row = lax.broadcasted_iota(jnp.int32, (128, 128), 0)
    lane = lax.broadcasted_iota(jnp.int32, (128, 128), 1)
    home = jnp.where(row < n_blocks, bricks >> 10, -1)
    home_t = jnp.transpose(home.astype(jnp.float32)).astype(jnp.int32)
    rank = jnp.sum(
        jnp.where((home == home_t) & (lane < row), 1.0, 0.0), axis=1, keepdims=True
    ).astype(jnp.int32)
    slot = jnp.where(row < n_blocks, 2 * home + rank, -1)
    slot_t = jnp.transpose(slot.astype(jnp.float32)).astype(jnp.int32)
    by = (bricks >> 5) & 31
    place = ((by >> 4) * 64 + (bricks & 3) * 16 + (by & 15) + 1).astype(jnp.bfloat16)
    slot_row = lax.broadcasted_iota(jnp.int32, (2 * n_wide, 128), 0)
    slot_row = jnp.where(slot_row < n_wide, 2 * slot_row, 2 * (slot_row - n_wide) + 1)
    pick = jnp.where(
        jnp.broadcast_to(slot_t[0:1], (2 * n_wide, 128)) == slot_row, 1.0, 0.0
    ).astype(jnp.bfloat16)[:, :32]
    first = lax.broadcasted_iota(jnp.int32, (32, 128), 1) < 64
    places = jnp.dot(pick, place[:32], preferred_element_type=jnp.float32) - 1.0
    place_send[:, 0, :] = jnp.where(first, places[:n_wide], places[n_wide:])
    pick = jnp.concatenate([pick, pick], 1)

    loads[2].wait()
    loads[3].wait()
    for g in range(waves_ref.shape[0]):
        at = slice(g * GRP, g * GRP + GRP)
        waves_ref[g, 0:3, :] = freq_ref[:, at]
        waves_ref[g, 3:6, :] = phase_ref[:, at]
        waves_ref[g, 6:8, :] = jnp.zeros((2, GRP), jnp.float32)
    piece_ref[...] = jnp.zeros_like(piece_ref)

    def prepare(b, carry):
        block_factors(b, groups_ref, brick_ref, waves_ref, factor_ref)
        return carry

    lax.fori_loop(0, n_blocks, prepare, 0, unroll=4)
    loads[4].wait()
    for load in loads[5:]:
        load.start()

    def halve(b, carry):
        block_halves(b, blocks_ref, weight_ref)
        return carry

    lax.fori_loop(0, n_blocks, halve, 0, unroll=4)

    def place_copy(d):
        peer = lax.rem(wide + d, n_wide)
        return pltpu.make_async_remote_copy(
            src_ref=place_send.at[peer],
            dst_ref=place_recv.at[wide],
            send_sem=place_ssem,
            recv_sem=place_rsem,
            device_id=(peer, narrow),
            device_id_type=MESH,
        )

    def piece_copy(h, d):
        peer = lax.rem(wide + d, n_wide)
        return pltpu.make_async_remote_copy(
            src_ref=send_ref.at[h, pl.ds(pl.multiple_of(peer * 8, 8), 8)],
            dst_ref=recv_ref.at[h, pl.ds(pl.multiple_of(wide * 8, 8), 8)],
            send_sem=piece_ssem.at[h],
            recv_sem=piece_rsem.at[h],
            device_id=(peer, narrow),
            device_id_type=MESH,
        )

    own8 = pl.ds(pl.multiple_of(wide * 8, 8), 8)

    def compute_half(h):
        def work(b, carry):
            piece_ref[h, pl.ds(pl.multiple_of(b * 8, 8), 8), :] = half_piece(
                b, h, factor_ref, weight_ref
            )
            return carry

        lax.fori_loop(0, n_blocks, work, 0, unroll=8)
        rows = [piece_ref[h, pl.ds(r, 32, stride=8), :] for r in range(8)]
        both = jnp.concatenate(split(jnp.concatenate(rows, 1)), 0)
        slots = jnp.dot(pick, both, preferred_element_type=jnp.float32)
        for r in range(8):
            at = slice(r * 128, r * 128 + 128)
            send_ref[h, pl.ds(r, n_wide, stride=8), :] = jnp.where(
                first, slots[:n_wide, at], slots[n_wide:, at]
            )

    def send_half(h):
        def start_piece(d, carry):
            piece_copy(h, d).start()
            return carry

        lax.fori_loop(1, n_wide, start_piece, 0)
        recv_ref[h, own8] = send_ref[h, own8]

    compute_half(0)
    pl.semaphore_wait(barrier, n_wide + n_narrow - 2)
    send_half(0)

    def start_place(d, carry):
        place_copy(d).start()
        return carry

    lax.fori_loop(1, n_wide, start_place, 0)
    place_recv[wide] = place_send[wide]

    loads[5].wait()
    at = lax.broadcasted_iota(jnp.int32, (256, 256), 0)
    to = (
        ((at >> 4) & 1) * 128 + (at >> 7) * 64 + ((at >> 5) & 3) * 16 + (at & 15)
    )
    order = jnp.where(
        to == lax.broadcasted_iota(jnp.int32, (256, 256), 1), 1.0, 0.0
    ).astype(jnp.bfloat16)
    for r in range(4):
        rows = []
        for g in range(8):
            y = g % 4 * 8 + 2 * r + g // 4
            rows.append(
                jnp.concatenate(
                    [core_ref[pl.ds(y + t * 512, 16, stride=32), :] for t in range(2)],
                    1,
                )
            )
        value = jnp.concatenate(rows, 0)
        high, rest = value.astype(jnp.bfloat16), value
        rest = rest - high.astype(jnp.float32)
        moved = (
            jnp.dot(high, order, preferred_element_type=jnp.float32)
            + sum(
                jnp.dot(part, order, preferred_element_type=jnp.float32)
                for part in split(rest)
            )
        )
        for h in range(2):
            own = moved[:, h * 128 : h * 128 + 128]
            core_part[h, r * 128 : r * 128 + 128, :] = own
            core_pow[h, r * 128 : r * 128 + 128, :] = power43(own)

    compute_half(1)
    send_half(1)
    wait_all(place_recv.at[pl.ds(0, n_wide - 1)], place_rsem)
    wait_all(place_send.at[pl.ds(0, n_wide - 1)], place_ssem)
    places = place_recv[:, 0, :]
    brick_lane = lax.broadcasted_iota(jnp.int32, (n_wide, 128), 1).astype(jnp.float32)
    spots = [
        jnp.where(places[:, k * 64 : k * 64 + 1] == brick_lane, 1.0, 0.0)
        for k in range(2)
    ]
    gather = jnp.transpose(jnp.concatenate([*spots, *spots], 0)).astype(jnp.bfloat16)

    chips = n_narrow // 2
    hops = [(1, 0), (3, 0), (1, 1), (3, 1), (2, 0), (2, 1), (0, 1), (0, 0)]

    def peer_at(hop):
        chip = lax.rem(narrow // 2 + hop[0], chips)
        return chip * 2 + lax.rem(narrow + hop[1], 2)

    def half_copy(h, i):
        peer = peer_at(hops[i])
        return pltpu.make_async_remote_copy(
            src_ref=half_send.at[h, peer],
            dst_ref=half_recv.at[h, narrow],
            send_sem=half_ssem.at[h, i],
            recv_sem=half_rsem.at[h, i],
            device_id=(wide, peer),
            device_id_type=MESH,
        )

    group = lax.broadcasted_iota(jnp.int32, (16, 128), 1) >> 4
    low16 = group < 4
    low64 = lax.broadcasted_iota(jnp.int32, (64, 128), 1) < 64
    for h in range(2):
        others = pl.ds(0, (n_wide - 1) * 8)
        wait_all(recv_ref.at[h, others], piece_rsem.at[h])
        wait_all(send_ref.at[h, others], piece_ssem.at[h])
        halves = []
        for r in range(4):
            even = recv_ref[h, pl.ds(2 * r, n_wide, stride=8), :]
            odd = recv_ref[h, pl.ds(2 * r + 1, n_wide, stride=8), :]
            got = jnp.concatenate(
                [
                    jnp.where(first, even, pltpu.roll(odd, 64, 1)),
                    jnp.where(first, pltpu.roll(even, 64, 1), odd),
                ],
                0,
            )
            halves.append(jnp.concatenate(split(got), 0))
        all_sums = jnp.dot(
            gather, jnp.concatenate(halves, 1), preferred_element_type=jnp.float32
        )
        for r in range(4):
            sums = all_sums[:, r * 128 : r * 128 + 128]
            tiles = [sums[j * 16 : j * 16 + 16] for j in range(8)]
            for bit in (1, 2, 4):
                for j in range(8):
                    if not j & bit:
                        a, b = tiles[j], tiles[j | bit]
                        keep = (group & bit) == 0
                        tiles[j] = jnp.where(keep, a, pltpu.roll(b, 16 * bit, 1))
                        tiles[j | bit] = jnp.where(
                            keep, pltpu.roll(a, 128 - 16 * bit, 1), b
                        )
            for g in range(8):
                at = slice((r * 8 + g) * 16, (r * 8 + g) * 16 + 16)
                rho = core_part[h, at, :] + tiles[g]
                energy = energy_coef * (power43(jnp.abs(rho)) - core_pow[h, at, :])
                other = pltpu.roll(energy, 64, 1)
                fold = jnp.where(low16, energy + other, other - energy)
                high = fold.astype(jnp.bfloat16).astype(jnp.float32)
                rest = fold - high
                fold_ref[h, 0, at, :] = jnp.where(
                    low16, high, pltpu.roll(rest, 64, 1)
                ).astype(jnp.bfloat16)
                fold_ref[h, 1, at, :] = jnp.where(
                    low16, pltpu.roll(high, 64, 1), rest
                ).astype(jnp.bfloat16)
        if h == 0:
            loads[6].wait()
        for i, hop in enumerate(hops):
            peer = peer_at(hop)
            target = half_recv.at[h, narrow] if hop == (0, 0) else half_send.at[h, peer]
            for parity in range(2):
                half = jnp.dot(
                    ytab_ref[0, peer, parity],
                    fold_ref[h, parity],
                    preferred_element_type=jnp.float32,
                ) + jnp.dot(
                    ytab_ref[1, peer, parity],
                    fold_ref[h, parity],
                    preferred_element_type=jnp.float32,
                )
                half = half + pltpu.roll(half, 64, 1)
                target[pl.ds(parity, 64, stride=2), :] = jnp.where(
                    low64, half[:64], half[64:]
                )
            if hop != (0, 0):
                half_copy(h, i).start()

    loads[7].wait()
    low256 = (lax.broadcasted_iota(jnp.int32, (128, 256), 1) & 127) < 64
    waits = {0: (6,), 1: (1, 3), 3: (0, 2), 2: (4, 5)}
    for h in range(2):
        for on, copies in waits.items():
            for i in copies:
                half_copy(h, i).wait_recv()
            chip = lax.rem(narrow // 2 + on, chips)
            ours = [half_recv[h, 2 * chip + core] for core in range(2)]
            turned = [pltpu.roll(own, 64, 1) for own in ours]
            real, imag = jnp.concatenate(ours, 1), jnp.concatenate(turned, 1)
            high, low = split(
                jnp.concatenate([real, jnp.where(low256, imag, -imag)], 0)
            )
            part = (
                jnp.dot(high, xtab_ref[0, h, chip], preferred_element_type=jnp.float32)
                + jnp.dot(low, xtab_ref[0, h, chip], preferred_element_type=jnp.float32)
                + jnp.dot(high, xtab_ref[1, h, chip], preferred_element_type=jnp.float32)
            )
            if (h, on) == (0, 0):
                acc_ref[...] = part
            elif (h, on) != (1, 2):
                acc_ref[...] += part
            else:
                total = acc_ref[...] + part
                for c in range(2):
                    out_ref[0, c] = total[c * 128 : c * 128 + 128]

    for h in range(2):
        for i in range(len(hops) - 1):
            half_copy(h, i).wait_send()


def local(density_blocks, block_groups, block_brick, orbital_freq, orbital_phase, core_density):
    n_wide, n_narrow = lax.axis_size("wide"), lax.axis_size("narrow")
    n_blocks = density_blocks.shape[0]
    ytab, xtab = y_tables(n_narrow), x_tables(n_narrow // 2)
    vmem = pl.BlockSpec(memory_space=pltpu.VMEM)
    hbm = pl.BlockSpec(memory_space=pltpu.HBM)
    f32, bf16 = jnp.float32, jnp.bfloat16
    rows = NY // n_narrow
    return pl.pallas_call(
        functools.partial(whole_kernel, n_wide, n_narrow, n_blocks),
        out_shape=jax.ShapeDtypeStruct((1, 2, rows, NX // 2), f32),
        in_specs=[hbm] * 8,
        out_specs=vmem,
        scratch_shapes=[
            pltpu.SMEM((2, n_blocks), jnp.int32),
            pltpu.SMEM((n_blocks,), jnp.int32),
            pltpu.VMEM(orbital_freq.shape, f32),
            pltpu.VMEM(orbital_phase.shape, f32),
            pltpu.VMEM(density_blocks.shape, f32),
            pltpu.VMEM(core_density.shape[1:], f32),
            pltpu.VMEM(ytab.shape, bf16),
            pltpu.VMEM(xtab.shape, bf16),
            pltpu.VMEM((orbital_freq.shape[1] // GRP, 8, GRP), f32),
            pltpu.VMEM((n_blocks, 4, 32, GRP), f32),
            pltpu.VMEM((n_blocks, 2 * GRP, 2 * GRP), bf16),
            pltpu.VMEM((128, 128), jnp.int32),
            pltpu.VMEM((2, 32 * 8, 128), f32),
            pltpu.VMEM((n_wide, 1, 128), f32),
            pltpu.VMEM((n_wide, 1, 128), f32),
            pltpu.VMEM((2, n_wide * 8, 128), f32),
            pltpu.VMEM((2, n_wide * 8, 128), f32),
            pltpu.VMEM((2, NY // 2, 128), f32),
            pltpu.VMEM((2, NY // 2, 128), f32),
            pltpu.VMEM((2, 2, NY // 2, 128), bf16),
            pltpu.VMEM((2, n_narrow, 128, 128), f32),
            pltpu.VMEM((2, n_narrow, 128, 128), f32),
            pltpu.VMEM((256, NX // 2), f32),
            pltpu.SemaphoreType.DMA((8,)),
            pltpu.SemaphoreType.DMA,
            pltpu.SemaphoreType.DMA,
            pltpu.SemaphoreType.DMA((2,)),
            pltpu.SemaphoreType.DMA((2,)),
            pltpu.SemaphoreType.DMA((2, n_narrow)),
            pltpu.SemaphoreType.DMA((2, n_narrow)),
        ],
        compiler_params=pltpu.CompilerParams(
            collective_id=0, has_side_effects=True, vmem_limit_bytes=48 * 2**20
        ),
    )(
        *(
            pltpu.with_memory_space_constraint(array, pltpu.HBM)
            for array in (
                block_groups.T,
                block_brick,
                orbital_freq,
                orbital_phase,
                density_blocks,
                core_density.reshape(core_density.shape[1:]),
                jnp.asarray(ytab),
                jnp.asarray(xtab),
            )
        ),
    )


def solution(mesh):
    return jax.shard_map(
        local,
        mesh=mesh,
        in_specs=(
            P(("wide", "narrow"), None, None),
            P(("wide", "narrow"), None),
            P(("wide", "narrow")),
            P(),
            P(),
            P("wide", None, "narrow"),
        ),
        out_specs=P("wide", None, "narrow", None),
        check_vma=False,
    )
```

```python
import functools
import math

import jax
import jax.numpy as jnp
import ml_dtypes
import numpy as np
from jax import lax
from jax.experimental import pallas as pl
from jax.experimental.pallas import tpu as pltpu
from jax.sharding import PartitionSpec as P

NX = 1024
NY = 1024
GRP = 128
BY = 32
BX = 32
MESH = pl.DeviceIdType.MESH

energy_coef = -0.75 * (3.0 / math.pi) ** (1.0 / 3.0)

INV_TURN = 1.0 / (2.0 * math.pi)
PI_HI = 3.140625
PI_LO = math.pi - PI_HI
SINE = (
    2.604579135698264e-06,
    -0.00019808792785020506,
    0.008333047269825162,
    -0.16666657833027024,
    0.9999999956345141,
)


def cosine(angle):
    turns = jnp.round(angle * INV_TURN)
    half = (0.5 * angle - turns * PI_HI) - turns * PI_LO
    square = half * half
    poly = SINE[0]
    for coef in SINE[1:]:
        poly = poly * square + coef
    sine = half * poly
    return 1.0 - 2.0 * (sine * sine)


def split(value):
    high = value.astype(jnp.bfloat16)
    return high, (value - high.astype(jnp.float32)).astype(jnp.bfloat16)


def power43(value):
    return jnp.exp(jnp.log(value) * (4.0 / 3.0))


def split_table(table):
    table = np.asarray(table, np.float32)
    high = table.astype(ml_dtypes.bfloat16)
    low = (table - high.astype(np.float32)).astype(ml_dtypes.bfloat16)
    return np.stack([high, low])


def y_tables(parts):
    rows = NY // parts
    col = np.arange(NY // 2)
    r, g = col // 128, col // 16 % 8
    y = col % 16 * 32 + g % 4 * 8 + 2 * r + g // 4
    ky = (
        np.arange(parts)[:, None, None] * rows
        + np.arange(2)[None, :, None]
        + 2 * np.arange(rows // 2)[None, None, :]
    )
    angle = 2.0 * np.pi / NY * (ky[..., None] * y % NY)
    return split_table(
        np.concatenate([np.cos(angle), -np.sin(angle)], 2) / math.sqrt(NY)
    )


def x_tables(chips):
    h, chip, core, xb, xi = np.ix_(*map(np.arange, (2, chips, 2, 4, 16)))
    x = (chip * 2 + core) * 128 + xb * 32 + h * 16 + xi
    x = x.reshape(2, chips, 2, 64, 1)
    angle = 2.0 * np.pi / NX * (x * np.arange(NX // 2) % NX)
    both = np.stack([np.cos(angle), np.sin(angle)], 3) / math.sqrt(NX)
    return split_table(both.reshape(2, chips, 256, NX // 2))


def wait_all(ref, sem):
    pltpu.make_async_copy(ref, ref, sem).wait()


def block_factors(b, groups_ref, brick_ref, waves_ref, factor_ref):
    brick = brick_ref[b]
    x0 = ((brick & 31) * BX).astype(jnp.float32)
    y0 = (((brick >> 5) & 31) * BY).astype(jnp.float32)
    z0 = (brick >> 10).astype(jnp.float32)
    step = lax.broadcasted_iota(jnp.int32, (32, GRP), 0).astype(jnp.float32)
    xs, ys = step + x0, step + y0
    for side in range(2):
        wave = waves_ref[groups_ref[side, b]]
        along_z = cosine(z0 * wave[2:3] + wave[5:6])
        factor_ref[b, 2 * side] = cosine(xs * wave[0:1] + wave[3:4]) * along_z
        factor_ref[b, 2 * side + 1] = cosine(ys * wave[1:2] + wave[4:5])


def block_halves(b, blocks_ref, weight_ref):
    high, low = split(blocks_ref[b])
    weight_ref[b] = jnp.concatenate(
        [
            jnp.concatenate([high, low], 1),
            jnp.concatenate([high, jnp.zeros_like(low)], 1),
        ],
        0,
    )


def half_piece(b, h, factor_ref, weight_ref):
    cols = slice(h * 16, h * 16 + 16)
    left_x, right_x = factor_ref[b, 0, cols], factor_ref[b, 2, cols]
    weights = weight_ref[b]
    shape = (2, 16, 8, GRP)
    lane = lax.broadcasted_iota(jnp.int32, shape, 3) & 63
    spot = lax.broadcasted_iota(jnp.int32, shape, 1) + 16 * lax.broadcasted_iota(
        jnp.int32, shape, 0
    )
    total = jnp.zeros((8, 128), jnp.float32)
    for part in range(2):
        rows = slice(part * 16, part * 16 + 16)
        left_y = factor_ref[b, 1, rows].reshape(2, 1, 8, GRP)
        right_y = factor_ref[b, 3, rows].reshape(2, 1, 8, GRP)
        left = (left_x[None, :, None, :] * left_y).reshape(256, GRP)
        right = right_x[None, :, None, :] * right_y
        mixed = jnp.dot(
            jnp.concatenate(split(left), 1), weights, preferred_element_type=jnp.float32
        )
        mixed = (mixed[:, :GRP] + mixed[:, GRP:]).reshape(shape) * right
        sums = jnp.sum(mixed, axis=3, keepdims=True)
        total = total + jnp.sum(
            jnp.where(lane == spot + part * 32, sums, 0.0), axis=(0, 1)
        )
    return total


def whole_kernel(
    n_wide,
    n_narrow,
    n_blocks,
    groups_hbm,
    brick_hbm,
    freq_hbm,
    phase_hbm,
    blocks_hbm,
    core_hbm,
    ytab_hbm,
    xtab_hbm,
    out_ref,
    groups_ref,
    brick_ref,
    freq_ref,
    phase_ref,
    blocks_ref,
    core_ref,
    ytab_ref,
    xtab_ref,
    waves_ref,
    factor_ref,
    weight_ref,
    brick_col,
    piece_ref,
    place_send,
    place_recv,
    send_ref,
    recv_ref,
    core_part,
    core_pow,
    fold_ref,
    half_send,
    half_recv,
    acc_ref,
    load_sem,
    place_ssem,
    place_rsem,
    piece_ssem,
    piece_rsem,
    half_ssem,
    half_rsem,
):
    wide, narrow = lax.axis_index("wide"), lax.axis_index("narrow")
    loads = [
        pltpu.make_async_copy(src, dst, load_sem.at[i])
        for i, (src, dst) in enumerate(
            (
                (brick_hbm, brick_ref),
                (groups_hbm, groups_ref),
                (freq_hbm, freq_ref),
                (phase_hbm, phase_ref),
                (blocks_hbm, blocks_ref),
                (core_hbm, core_ref),
                (ytab_hbm, ytab_ref),
                (xtab_hbm, xtab_ref),
            )
        )
    ]
    for load in loads[:5]:
        load.start()

    barrier = pltpu.get_barrier_semaphore()

    def greet_wide(d, carry):
        peer = lax.rem(wide + d, n_wide)
        pl.semaphore_signal(
            barrier, inc=1, device_id=(peer, narrow), device_id_type=MESH
        )
        return carry

    def greet_narrow(d, carry):
        peer = lax.rem(narrow + d, n_narrow)
        pl.semaphore_signal(
            barrier, inc=1, device_id=(wide, peer), device_id_type=MESH
        )
        return carry

    lax.fori_loop(1, n_wide, greet_wide, 0)
    lax.fori_loop(1, n_narrow, greet_narrow, 0)

    loads[0].wait()
    loads[1].wait()
    brick_col[...] = jnp.zeros_like(brick_col)

    def spread(b, carry):
        brick_col[pl.ds(b, 1), :] = jnp.full((1, 128), brick_ref[b], jnp.int32)
        return carry

    lax.fori_loop(0, n_blocks, spread, 0)
    bricks = brick_col[...]
    row = lax.broadcasted_iota(jnp.int32, (128, 128), 0)
    lane = lax.broadcasted_iota(jnp.int32, (128, 128), 1)
    home = jnp.where(row < n_blocks, bricks >> 10, -1)
    home_t = jnp.transpose(home.astype(jnp.float32)).astype(jnp.int32)
    rank = jnp.sum(
        jnp.where((home == home_t) & (lane < row), 1.0, 0.0), axis=1, keepdims=True
    ).astype(jnp.int32)
    slot = jnp.where(row < n_blocks, 2 * home + rank, -1)
    slot_t = jnp.transpose(slot.astype(jnp.float32)).astype(jnp.int32)
    by = (bricks >> 5) & 31
    place = ((by >> 4) * 64 + (bricks & 3) * 16 + (by & 15) + 1).astype(jnp.bfloat16)
    slot_row = lax.broadcasted_iota(jnp.int32, (2 * n_wide, 128), 0)
    slot_row = jnp.where(slot_row < n_wide, 2 * slot_row, 2 * (slot_row - n_wide) + 1)
    pick = jnp.where(
        jnp.broadcast_to(slot_t[0:1], (2 * n_wide, 128)) == slot_row, 1.0, 0.0
    ).astype(jnp.bfloat16)[:, :32]
    first = lax.broadcasted_iota(jnp.int32, (32, 128), 1) < 64
    places = jnp.dot(pick, place[:32], preferred_element_type=jnp.float32) - 1.0
    place_send[:, 0, :] = jnp.where(first, places[:n_wide], places[n_wide:])
    pick = jnp.concatenate([pick, pick], 1)

    loads[2].wait()
    loads[3].wait()
    for g in range(waves_ref.shape[0]):
        at = slice(g * GRP, g * GRP + GRP)
        waves_ref[g, 0:3, :] = freq_ref[:, at]
        waves_ref[g, 3:6, :] = phase_ref[:, at]
        waves_ref[g, 6:8, :] = jnp.zeros((2, GRP), jnp.float32)
    piece_ref[...] = jnp.zeros_like(piece_ref)

    def prepare(b, carry):
        block_factors(b, groups_ref, brick_ref, waves_ref, factor_ref)
        return carry

    lax.fori_loop(0, n_blocks, prepare, 0, unroll=4)
    loads[4].wait()
    for load in loads[5:]:
        load.start()

    def halve(b, carry):
        block_halves(b, blocks_ref, weight_ref)
        return carry

    lax.fori_loop(0, n_blocks, halve, 0, unroll=4)

    def place_copy(d):
        peer = lax.rem(wide + d, n_wide)
        return pltpu.make_async_remote_copy(
            src_ref=place_send.at[peer],
            dst_ref=place_recv.at[wide],
            send_sem=place_ssem,
            recv_sem=place_rsem,
            device_id=(peer, narrow),
            device_id_type=MESH,
        )

    def piece_copy(h, d):
        peer = lax.rem(wide + d, n_wide)
        return pltpu.make_async_remote_copy(
            src_ref=send_ref.at[h, pl.ds(pl.multiple_of(peer * 8, 8), 8)],
            dst_ref=recv_ref.at[h, pl.ds(pl.multiple_of(wide * 8, 8), 8)],
            send_sem=piece_ssem.at[h],
            recv_sem=piece_rsem.at[h],
            device_id=(peer, narrow),
            device_id_type=MESH,
        )

    own8 = pl.ds(pl.multiple_of(wide * 8, 8), 8)

    def compute_half(h):
        def work(b, carry):
            piece_ref[h, pl.ds(pl.multiple_of(b * 8, 8), 8), :] = half_piece(
                b, h, factor_ref, weight_ref
            )
            return carry

        lax.fori_loop(0, n_blocks, work, 0, unroll=8)
        rows = [piece_ref[h, pl.ds(r, 32, stride=8), :] for r in range(8)]
        both = jnp.concatenate(split(jnp.concatenate(rows, 1)), 0)
        slots = jnp.dot(pick, both, preferred_element_type=jnp.float32)
        for r in range(8):
            at = slice(r * 128, r * 128 + 128)
            send_ref[h, pl.ds(r, n_wide, stride=8), :] = jnp.where(
                first, slots[:n_wide, at], slots[n_wide:, at]
            )

    def send_half(h):
        def start_piece(d, carry):
            piece_copy(h, d).start()
            return carry

        lax.fori_loop(1, n_wide, start_piece, 0)
        recv_ref[h, own8] = send_ref[h, own8]

    compute_half(0)
    pl.semaphore_wait(barrier, n_wide + n_narrow - 2)
    send_half(0)

    def start_place(d, carry):
        place_copy(d).start()
        return carry

    lax.fori_loop(1, n_wide, start_place, 0)
    place_recv[wide] = place_send[wide]

    loads[5].wait()
    at = lax.broadcasted_iota(jnp.int32, (256, 256), 0)
    to = (
        ((at >> 4) & 1) * 128 + (at >> 7) * 64 + ((at >> 5) & 3) * 16 + (at & 15)
    )
    order = jnp.where(
        to == lax.broadcasted_iota(jnp.int32, (256, 256), 1), 1.0, 0.0
    ).astype(jnp.bfloat16)
    for r in range(4):
        rows = []
        for g in range(8):
            y = g % 4 * 8 + 2 * r + g // 4
            rows.append(
                jnp.concatenate(
                    [core_ref[pl.ds(y + t * 512, 16, stride=32), :] for t in range(2)],
                    1,
                )
            )
        value = jnp.concatenate(rows, 0)
        high, rest = value.astype(jnp.bfloat16), value
        rest = rest - high.astype(jnp.float32)
        moved = (
            jnp.dot(high, order, preferred_element_type=jnp.float32)
            + sum(
                jnp.dot(part, order, preferred_element_type=jnp.float32)
                for part in split(rest)
            )
        )
        for h in range(2):
            own = moved[:, h * 128 : h * 128 + 128]
            core_part[h, r * 128 : r * 128 + 128, :] = own
            core_pow[h, r * 128 : r * 128 + 128, :] = power43(own)

    compute_half(1)
    send_half(1)
    wait_all(place_recv.at[pl.ds(0, n_wide - 1)], place_rsem)
    places = place_recv[:, 0, :]
    brick_lane = lax.broadcasted_iota(jnp.int32, (n_wide, 128), 1).astype(jnp.float32)
    spots = [
        jnp.where(places[:, k * 64 : k * 64 + 1] == brick_lane, 1.0, 0.0)
        for k in range(2)
    ]
    gather = jnp.transpose(jnp.concatenate([*spots, *spots], 0)).astype(jnp.bfloat16)

    chips = n_narrow // 2
    hops = [(1, 0), (3, 0), (1, 1), (3, 1), (2, 0), (2, 1), (0, 1), (0, 0)]

    def peer_at(hop):
        chip = lax.rem(narrow // 2 + hop[0], chips)
        return chip * 2 + lax.rem(narrow + hop[1], 2)

    def half_copy(h, i):
        peer = peer_at(hops[i])
        return pltpu.make_async_remote_copy(
            src_ref=half_send.at[h, peer],
            dst_ref=half_recv.at[h, narrow],
            send_sem=half_ssem.at[h, i],
            recv_sem=half_rsem.at[h, i],
            device_id=(wide, peer),
            device_id_type=MESH,
        )

    group = lax.broadcasted_iota(jnp.int32, (16, 128), 1) >> 4
    low16 = group < 4
    low64 = lax.broadcasted_iota(jnp.int32, (64, 128), 1) < 64
    for h in range(2):
        others = pl.ds(0, (n_wide - 1) * 8)
        wait_all(recv_ref.at[h, others], piece_rsem.at[h])
        halves = []
        for r in range(4):
            even = recv_ref[h, pl.ds(2 * r, n_wide, stride=8), :]
            odd = recv_ref[h, pl.ds(2 * r + 1, n_wide, stride=8), :]
            got = jnp.concatenate(
                [
                    jnp.where(first, even, pltpu.roll(odd, 64, 1)),
                    jnp.where(first, pltpu.roll(even, 64, 1), odd),
                ],
                0,
            )
            halves.append(jnp.concatenate(split(got), 0))
        all_sums = jnp.dot(
            gather, jnp.concatenate(halves, 1), preferred_element_type=jnp.float32
        )
        for r in range(4):
            sums = all_sums[:, r * 128 : r * 128 + 128]
            tiles = [sums[j * 16 : j * 16 + 16] for j in range(8)]
            for bit in (1, 2, 4):
                for j in range(8):
                    if not j & bit:
                        a, b = tiles[j], tiles[j | bit]
                        keep = (group & bit) == 0
                        tiles[j] = jnp.where(keep, a, pltpu.roll(b, 16 * bit, 1))
                        tiles[j | bit] = jnp.where(
                            keep, pltpu.roll(a, 128 - 16 * bit, 1), b
                        )
            for g in range(8):
                at = slice((r * 8 + g) * 16, (r * 8 + g) * 16 + 16)
                rho = core_part[h, at, :] + tiles[g]
                energy = energy_coef * (power43(jnp.abs(rho)) - core_pow[h, at, :])
                other = pltpu.roll(energy, 64, 1)
                fold = jnp.where(low16, energy + other, other - energy)
                high = fold.astype(jnp.bfloat16).astype(jnp.float32)
                rest = fold - high
                fold_ref[h, 0, at, :] = jnp.where(
                    low16, high, pltpu.roll(rest, 64, 1)
                ).astype(jnp.bfloat16)
                fold_ref[h, 1, at, :] = jnp.where(
                    low16, pltpu.roll(high, 64, 1), rest
                ).astype(jnp.bfloat16)
        if h == 0:
            loads[6].wait()
        for i, hop in enumerate(hops):
            peer = peer_at(hop)
            target = half_recv.at[h, narrow] if hop == (0, 0) else half_send.at[h, peer]
            for parity in range(2):
                half = jnp.dot(
                    ytab_ref[0, peer, parity],
                    fold_ref[h, parity],
                    preferred_element_type=jnp.float32,
                ) + jnp.dot(
                    ytab_ref[1, peer, parity],
                    fold_ref[h, parity],
                    preferred_element_type=jnp.float32,
                )
                half = half + pltpu.roll(half, 64, 1)
                target[pl.ds(parity, 64, stride=2), :] = jnp.where(
                    low64, half[:64], half[64:]
                )
            if hop != (0, 0):
                half_copy(h, i).start()

    loads[7].wait()
    low256 = (lax.broadcasted_iota(jnp.int32, (128, 256), 1) & 127) < 64
    waits = {0: (6,), 1: (1, 3), 3: (0, 2), 2: (4, 5)}
    for h in range(2):
        for on, copies in waits.items():
            for i in copies:
                half_copy(h, i).wait_recv()
            chip = lax.rem(narrow // 2 + on, chips)
            ours = [half_recv[h, 2 * chip + core] for core in range(2)]
            turned = [pltpu.roll(own, 64, 1) for own in ours]
            real, imag = jnp.concatenate(ours, 1), jnp.concatenate(turned, 1)
            high, low = split(
                jnp.concatenate([real, jnp.where(low256, imag, -imag)], 0)
            )
            part = (
                jnp.dot(high, xtab_ref[0, h, chip], preferred_element_type=jnp.float32)
                + jnp.dot(low, xtab_ref[0, h, chip], preferred_element_type=jnp.float32)
                + jnp.dot(high, xtab_ref[1, h, chip], preferred_element_type=jnp.float32)
            )
            if (h, on) == (0, 0):
                acc_ref[...] = part
            elif (h, on) != (1, 2):
                acc_ref[...] += part
            else:
                total = acc_ref[...] + part
                for c in range(2):
                    out_ref[0, c] = total[c * 128 : c * 128 + 128]

    wait_all(place_send.at[pl.ds(0, n_wide - 1)], place_ssem)
    for h in range(2):
        wait_all(send_ref.at[h, pl.ds(0, (n_wide - 1) * 8)], piece_ssem.at[h])
        for i in range(len(hops) - 1):
            half_copy(h, i).wait_send()


def local(density_blocks, block_groups, block_brick, orbital_freq, orbital_phase, core_density):
    n_wide, n_narrow = lax.axis_size("wide"), lax.axis_size("narrow")
    n_blocks = density_blocks.shape[0]
    ytab, xtab = y_tables(n_narrow), x_tables(n_narrow // 2)
    vmem = pl.BlockSpec(memory_space=pltpu.VMEM)
    hbm = pl.BlockSpec(memory_space=pltpu.HBM)
    f32, bf16 = jnp.float32, jnp.bfloat16
    rows = NY // n_narrow
    return pl.pallas_call(
        functools.partial(whole_kernel, n_wide, n_narrow, n_blocks),
        out_shape=jax.ShapeDtypeStruct((1, 2, rows, NX // 2), f32),
        in_specs=[hbm] * 8,
        out_specs=vmem,
        scratch_shapes=[
            pltpu.SMEM((2, n_blocks), jnp.int32),
            pltpu.SMEM((n_blocks,), jnp.int32),
            pltpu.VMEM(orbital_freq.shape, f32),
            pltpu.VMEM(orbital_phase.shape, f32),
            pltpu.VMEM(density_blocks.shape, f32),
            pltpu.VMEM(core_density.shape[1:], f32),
            pltpu.VMEM(ytab.shape, bf16),
            pltpu.VMEM(xtab.shape, bf16),
            pltpu.VMEM((orbital_freq.shape[1] // GRP, 8, GRP), f32),
            pltpu.VMEM((n_blocks, 4, 32, GRP), f32),
            pltpu.VMEM((n_blocks, 2 * GRP, 2 * GRP), bf16),
            pltpu.VMEM((128, 128), jnp.int32),
            pltpu.VMEM((2, 32 * 8, 128), f32),
            pltpu.VMEM((n_wide, 1, 128), f32),
            pltpu.VMEM((n_wide, 1, 128), f32),
            pltpu.VMEM((2, n_wide * 8, 128), f32),
            pltpu.VMEM((2, n_wide * 8, 128), f32),
            pltpu.VMEM((2, NY // 2, 128), f32),
            pltpu.VMEM((2, NY // 2, 128), f32),
            pltpu.VMEM((2, 2, NY // 2, 128), bf16),
            pltpu.VMEM((2, n_narrow, 128, 128), f32),
            pltpu.VMEM((2, n_narrow, 128, 128), f32),
            pltpu.VMEM((256, NX // 2), f32),
            pltpu.SemaphoreType.DMA((8,)),
            pltpu.SemaphoreType.DMA,
            pltpu.SemaphoreType.DMA,
            pltpu.SemaphoreType.DMA((2,)),
            pltpu.SemaphoreType.DMA((2,)),
            pltpu.SemaphoreType.DMA((2, n_narrow)),
            pltpu.SemaphoreType.DMA((2, n_narrow)),
        ],
        compiler_params=pltpu.CompilerParams(
            collective_id=0, has_side_effects=True, vmem_limit_bytes=48 * 2**20
        ),
    )(
        *(
            pltpu.with_memory_space_constraint(array, pltpu.HBM)
            for array in (
                block_groups.T,
                block_brick,
                orbital_freq,
                orbital_phase,
                density_blocks,
                core_density.reshape(core_density.shape[1:]),
                jnp.asarray(ytab),
                jnp.asarray(xtab),
            )
        ),
    )


def solution(mesh):
    return jax.shard_map(
        local,
        mesh=mesh,
        in_specs=(
            P(("wide", "narrow"), None, None),
            P(("wide", "narrow"), None),
            P(("wide", "narrow")),
            P(),
            P(),
            P("wide", None, "narrow"),
        ),
        out_specs=P("wide", None, "narrow", None),
        check_vma=False,
    )
```
